512 devices in a mesh: chan: 16 (over y_lo, z), frame: 32 (over x, y_hi, core).
Axes of the slice: x: 4, y: 8 (y_hi: 4, y_lo: 2; y = y_hi * 2 + y_lo), z: 8, core: 2. Of those that a mesh axis runs over, the one named last changes fastest.
Arguments:
- images: float32 [64, 32, 2, 256, 256], P('chan', 'frame'), may hold values from -6 to 6
- objects: float32 [64, 2, 256, 256], P('chan', None, 'frame'), may hold values from -24 to 24
- coeffs: float32 [32, 36], P('frame'), may hold values from -0.875 to 0.875
- mode_maps: float32 [36, 128, 128], P(None, 'chan'), may hold values from -4 to 4
- amplitude: float32 [128, 128], replicated, may hold values from 0.5 to 1.5
- phase_scale: float32 [64], P('chan'), may hold values from 0.6 to 1.2
Outputs:
- obj_grad: float32 [64, 2, 256, 256], P('chan', None, 'frame')
- mode_grad: float32 [32, 36], P('frame')
The draws below stay inside these ranges and needn't reach their ends.
All inputs are finite; a program needn't handle non-finite values.
Results may differ from the reference program's by a relative error of at most 0.0001.
Values sent between devices are 32-bit elements; how exact they have to be, the bound alone decides.
A program may use at most 64 MiB of HBM per device.

```python
import math
import jax
import jax.numpy as jnp
from jax import lax

GRID = 256
PUPIL = 128
MODES = 36
CH = 64
FRAMES = 32


def with_spikes(entries, stream_key, source, target, parts, factor):
    owner, partner = [(jnp.arange(entries.shape[axis_at]) // (entries.shape[axis_at] // parts)).reshape([-1 if axis == axis_at else 1 for axis in range(entries.ndim)]) for axis_at in (source, target)]
    chosen = jax.random.permutation(stream_key, parts)[partner]
    strong = (owner == chosen) | (owner == (partner + parts // 2) % parts)
    return jnp.where(strong, factor * entries, entries)


def level_of(rng, shape, pieces, low, largest):
    def one(position, parts):
        draws = jax.random.uniform(jax.random.fold_in(jax.random.fold_in(rng, 6), position), (parts,), jnp.float32, low / len(pieces), largest / len(pieces))
        return jnp.repeat(jnp.exp(draws), shape[position] // parts).reshape((-1,) + (1,) * (len(shape) - position - 1))

    level = one(*pieces[0])
    for cut in pieces[1:]:
        level = level * one(*cut)
    return level


def bell_draw(key, shape, width, reach, split=(), held_as=jnp.bfloat16):
    level = level_of(key, shape, split, -0.22, 0.18) if split else 1.0
    result = jax.random.normal(key, shape, jnp.float32) * width * level
    return jnp.minimum(jnp.maximum(result, -reach), reach).astype(held_as)


def heavy_noise(own_key, shape, deviation, most, cuts, heavy, dtype=jnp.bfloat16):
    drawn = deviation * jax.random.normal(own_key, shape, jnp.float32)
    if cuts:
        drawn = drawn * level_of(own_key, shape, cuts, -0.22, 0.18)
    return jnp.clip(with_spikes(drawn, jax.random.fold_in(own_key, 3), *heavy), -most, most).astype(dtype)


def setup_inputs(seed: int = 0) -> dict:
    keys = jax.random.split(jax.random.key(seed), 7)
    return {
        "images": heavy_noise(keys[0], (CH, FRAMES, 2, GRID, GRID), 1.0, 6.0, ((0, 16), (1, 32)), (1, 3, 32, 2.75), jnp.float32),
        "objects": bell_draw(keys[1], (CH, 2, GRID, GRID), 4.0, 24.0, ((0, 16), (2, 32)), jnp.float32),
        "coeffs": bell_draw(keys[2], (FRAMES, MODES), 0.15, 0.875, ((0, 32),), jnp.float32),
        "mode_maps": bell_draw(keys[3], (MODES, PUPIL, PUPIL), 1.0, 4.0, ((1, 16),), jnp.float32),
        "amplitude": jnp.clip(jax.random.uniform(keys[4], (PUPIL, PUPIL), jnp.float32, 0.5, 1.5), 0.5, 1.5),
        "phase_scale": jnp.clip(jnp.exp(math.log(1.2) - 0.6931472 * jax.random.uniform(keys[5], (CH,), jnp.float32) ** level_of(keys[5], (CH,), ((0, 16),), -0.2, 0.2)), 0.6, 1.2),
    }


HIGHEST = lax.Precision.HIGHEST


def circle_mask(extent):
    row_index = lax.broadcasted_iota(jnp.int32, (extent, extent), 0).astype(jnp.float32)
    col_index = lax.broadcasted_iota(jnp.int32, (extent, extent), 1).astype(jnp.float32)
    centre = (extent - 1) / 2.0
    radius = extent / 2.0
    inside = (row_index - centre) ** 2 + (col_index - centre) ** 2 <= radius * radius
    return jnp.where(inside, 1.0, 0.0).astype(jnp.float32)


def reference(images, objects, coeffs, mode_maps, amplitude, phase_scale):
    aperture = amplitude * circle_mask(PUPIL)
    psf_norm = (GRID * GRID) * jnp.sum(aperture * aperture)
    phases = jnp.einsum("km,mxy->kxy", coeffs, mode_maps, precision=HIGHEST)
    padding = ((0, 0), (0, GRID - PUPIL), (0, GRID - PUPIL))
    grid_area = float(GRID * GRID)

    def channel(running, slices):
        observed_all, object_pair, factor = slices
        angles = factor * phases
        pupil_field = aperture * jnp.cos(angles) + 1j * (aperture * jnp.sin(angles))
        spread = jnp.fft.fft2(jnp.pad(pupil_field, padding))
        psf_now = (jnp.real(spread) ** 2 + jnp.imag(spread) ** 2) / psf_norm
        transfer = jnp.fft.fft2(psf_now)
        object_now = object_pair[0] + 1j * object_pair[1]
        observed = observed_all[:, 0] + 1j * observed_all[:, 1]
        residual = object_now * transfer - observed
        object_term = jnp.sum(jnp.conj(transfer) * residual, axis=0)
        weight = jnp.conj(object_now) * residual
        along_psf = grid_area * jnp.real(jnp.fft.ifft2(weight))
        along_spread = (2.0 / psf_norm) * along_psf * spread
        along_field = grid_area * jnp.fft.ifft2(along_spread)[:, :PUPIL, :PUPIL]
        along_angle = jnp.imag(jnp.conj(pupil_field) * along_field)
        running = running + factor * along_angle
        return running, jnp.stack([jnp.real(object_term), jnp.imag(object_term)])

    initial = jnp.zeros((FRAMES, PUPIL, PUPIL), jnp.float32)
    phase_grad, obj_grad = lax.scan(channel, initial, (images, objects, phase_scale))
    mode_grad = jnp.einsum("kxy,mxy->km", phase_grad, mode_maps, precision=HIGHEST)
    return obj_grad, mode_grad
```

```python
import functools
import math

import jax
import jax.numpy as jnp
import ml_dtypes
import numpy as np
from jax import lax
from jax.experimental import pallas as pl
from jax.experimental.pallas import tpu as pltpu
from jax.sharding import PartitionSpec as P

F32 = jnp.float32
BF16 = jnp.bfloat16
MESH = pl.DeviceIdType.MESH
GRID = 256
PUPIL = 128
SECT = 2304

T_A, T_B, T_L2, T_H, T_C, T_S, T_HT, T_BACK = 0, 256, 512, 768, 1024, 1280, 1536, 1792


def build_tables():
    index = np.arange(GRID)
    turn = (np.outer(index, index) % GRID) * (2.0 * math.pi / GRID)
    cos, sin = np.cos(turn), np.sin(turn)
    half = PUPIL
    first = np.concatenate([cos[:half], sin[:half]], 0)
    second = np.concatenate([-sin[:half], cos[:half]], 0)
    left = np.concatenate([cos[:, :half], sin[:, :half]], 1)
    minus = -sin[:, :half]
    minus[:, 0] = cos[:, half]
    herm = np.concatenate([cos[:, :half], minus], 1)
    back = np.concatenate(
        [
            np.concatenate([cos[:, :half], sin[:, :half]], 1),
            np.concatenate([-sin[:, :half], cos[:, :half]], 1),
        ],
        0,
    )
    table = np.concatenate([first, second, left, herm, cos, sin, herm.T, back], 0).astype(np.float32)
    high = table.astype(ml_dtypes.bfloat16)
    high = high.astype(np.float32)
    low = (table - high).astype(ml_dtypes.bfloat16).astype(np.float32)
    return np.concatenate([high, low], 0)


def split(value):
    high = value.astype(BF16)
    low = (value - high.astype(F32)).astype(BF16)
    return high, low


def dot(a, b):
    return jnp.dot(a, b, preferred_element_type=F32)


def dot3(a_high, a_low, b_high, b_low):
    left = jnp.concatenate([a_high, a_low, a_high], 1)
    right = jnp.concatenate([b_high, b_high, b_low], 0)
    return dot(left, right)


def sincos(angle):
    k = jnp.floor(angle * (2.0 / math.pi) + 0.5)
    r = ((angle - k * 1.5703125) - k * 4.837512969970703125e-4) - k * 7.54978995489188216e-8
    z = r * r
    sin_r = ((-1.9515295891e-4 * z + 8.3321608736e-3) * z - 1.6666654611e-1) * z * r + r
    cos_r = ((2.443315711809948e-5 * z - 1.388731625493765e-3) * z + 4.166664568298827e-2) * z * z - 0.5 * z + 1.0
    quad = k - 4.0 * jnp.floor(k * 0.25)
    odd = (quad == 1.0) | (quad == 3.0)
    sin_v = jnp.where(odd, cos_r, sin_r)
    cos_v = jnp.where(odd, sin_r, cos_r)
    sin_v = jnp.where(quad >= 2.0, -sin_v, sin_v)
    cos_v = jnp.where((quad == 1.0) | (quad == 2.0), -cos_v, cos_v)
    return sin_v, cos_v


def mirror(value):
    lane = lax.broadcasted_iota(jnp.int32, value.shape, 1)
    index = (PUPIL - lane) & (PUPIL - 1)
    return jnp.take_along_axis(value, index, axis=1, mode="promise_in_bounds")


def kernel(
    n_chan,
    channels,
    modes,
    images_hbm,
    objects_hbm,
    coeffs_hbm,
    maps_hbm,
    amp_hbm,
    scale_hbm,
    table_hbm,
    grad_ref,
    mode_ref,
    coeffs,
    scale,
    maps,
    amp,
    img,
    tab,
    obj,
    term,
    land_a,
    land_b1,
    land_b2,
    land_c1,
    land_c2,
    phases,
    field,
    pupil,
    half,
    spread,
    otf,
    weight,
    along,
    pgrad,
    land_pg,
    part,
    vec,
    land_vec,
    local_sem,
    peer_send,
    peer_recv,
    g_send,
    g_recv,
    r_send,
    r_recv,
):
    pairs = channels // 2
    me = lax.axis_index("chan")
    fr = lax.axis_index("frame")
    cx = lax.div(fr, 8)
    cy = lax.rem(lax.div(fr, 2), 4)
    cc = lax.rem(fr, 2)
    x_r, x_l = lax.rem(cx + 1, 4), lax.rem(cx + 3, 4)
    y_r, y_l = lax.rem(cy + 1, 4), lax.rem(cy + 3, 4)
    sib = 1 - cc
    dev_xr = x_r * 8 + cy * 2 + cc
    dev_xl = x_l * 8 + cy * 2 + cc
    dev_yr = cx * 8 + y_r * 2 + cc
    dev_yl = cx * 8 + y_l * 2 + cc
    dev_sib = cx * 8 + cy * 2 + sib
    core_at = cc * 16
    sib_at = sib * 16

    class Order:
        def __init__(self, major, minor, devices):
            self.col, self.col_r, self.col_l, self.col_o = [
                core_at + lax.rem(major + step, 4) * 4 for step in (0, 1, 3, 2)
            ]
            self.own, self.own_r, self.own_l, self.own_o = [
                self.col + lax.rem(minor + step, 4) for step in (0, 1, 3, 2)
            ]
            self.major_r, self.major_l, self.minor_r, self.minor_l = devices

    by_column = Order(cx, cy, (dev_xr, dev_xl, dev_yr, dev_yl))
    by_row = Order(cy, cx, (dev_yr, dev_yl, dev_xr, dev_xl))
    last = channels - 1

    def order(j):
        return by_row if j == last else by_column

    def peer(step):
        return lax.rem(me + step, n_chan)

    def local(k, src, dst):
        copy = pltpu.make_async_copy(src, dst, local_sem.at[k])
        copy.start()
        return copy

    maps_copy = local(0, maps_hbm, maps)
    coeffs_copy = local(1, coeffs_hbm, coeffs)
    obj_copies = [
        local(2, objects_hbm.at[pl.ds(0, last)], obj.at[pl.ds(0, last), by_column.own]),
        local(7, objects_hbm.at[last], obj.at[last, by_row.own]),
    ]
    scale_copy = local(3, scale_hbm, scale)
    amp_copy = local(4, amp_hbm, amp)
    tab_copy = local(5, table_hbm, tab)
    img_copy = local(6, images_hbm, img)
    barrier = pltpu.get_barrier_semaphore()
    for dev in (dev_yr, dev_yl, dev_xr, dev_xl, dev_sib):
        pl.semaphore_signal(barrier, inc=1, device_id={"frame": dev}, device_id_type=MESH)
    for step in range(1, n_chan):
        pl.semaphore_signal(barrier, inc=1, device_id={"chan": peer(step)}, device_id_type=MESH)

    maps_copy.wait()
    coeffs_copy.wait()
    mine = coeffs[0, 0] * maps[0]
    for m in range(1, modes):
        mine = mine + coeffs[0, m] * maps[m]
    phases[me] = mine
    for copy in obj_copies:
        copy.wait()
    pl.semaphore_wait(barrier, 5 + n_chan - 1)

    def frame_copy(src, dst, send, recv, dev):
        return pltpu.make_async_remote_copy(
            src_ref=src,
            dst_ref=dst,
            send_sem=send,
            recv_sem=recv,
            device_id={"frame": dev},
            device_id_type=MESH,
        )

    def chan_copy(src, dst, phase, dev):
        return pltpu.make_async_remote_copy(
            src_ref=src,
            dst_ref=dst,
            send_sem=peer_send.at[phase],
            recv_sem=peer_recv.at[phase],
            device_id={"chan": dev},
            device_id_type=MESH,
        )

    def gather_start(j, stage):
        o = order(j)
        across = []
        if stage == 0:
            sent = [(obj.at[j, o.own], o.minor_r), (obj.at[j, o.own], o.minor_l)]
        elif stage == 1:
            sent = [(obj.at[j, o.own_l, 0], o.minor_r), (obj.at[j, o.own_r, 1], o.minor_l)]
        elif stage == 2:
            sent = [(obj.at[j, pl.ds(o.col, 4)], o.major_r), (obj.at[j, pl.ds(o.col, 4)], o.major_l)]
            across = [o.col]
        elif stage == 3:
            sent = [
                (obj.at[j, pl.ds(o.col_l, 2)], o.major_r),
                (obj.at[j, pl.ds(o.col_r + 2, 2)], o.major_l),
            ]
            across = [o.col_r, o.col_l]
        else:
            sent = []
            across = [o.col_o]
        for src, dev in sent:
            frame_copy(src, src, g_send.at[j], g_recv.at[j, stage], dev).start()
        for col in across:
            src = obj.at[j, pl.ds(col, 4)]
            frame_copy(src, src, g_send.at[j], g_recv.at[j, 4], dev_sib).start()

    def gather_wait(j, stage):
        blocks = obj.at[j, pl.ds(0, (2, 1, 8, 4, 16)[stage])]
        frame_copy(blocks, blocks, g_send.at[j], g_recv.at[j, stage], dev_sib).wait_recv()

    def gather_next(j, stage):
        gather_wait(j, stage)
        gather_start(j, stage + 1)

    groups = ((0, 2), (2, 1), (3, 1))

    def reduce_start(g, stage):
        first, count = groups[g]
        o = order(first)
        here = pl.ds(first, count)
        if stage == 0:
            sent = [
                (term.at[here, pl.ds(sib_at + col, 4)], land_a.at[here, pl.ds(col, 4)], dev_sib)
                for col in [at - core_at for at in (o.col_o, o.col_r, o.col_l, o.col)]
            ]
        elif stage == 1:
            sent = [
                (term.at[here, pl.ds(o.col_o, 2)], land_b1.at[0, here], o.major_r),
                (term.at[here, pl.ds(o.col_o + 2, 2)], land_b1.at[1, here], o.major_l),
            ]
        elif stage == 2:
            sent = [
                (term.at[here, pl.ds(o.col_r, 4)], land_b2.at[0, here], o.major_r),
                (term.at[here, pl.ds(o.col_l, 4)], land_b2.at[1, here], o.major_l),
            ]
        elif stage == 3:
            sent = [
                (term.at[here, o.own_o, 0], land_c1.at[0, here], o.minor_r),
                (term.at[here, o.own_o, 1], land_c1.at[1, here], o.minor_l),
            ]
        else:
            sent = [
                (term.at[here, o.own_r], land_c2.at[0, here], o.minor_r),
                (term.at[here, o.own_l], land_c2.at[1, here], o.minor_l),
            ]
        for src, land, dev in sent:
            frame_copy(src, land, r_send.at[g], r_recv.at[g, stage], dev).start()

    def reduce_finish(g, stage):
        first, count = groups[g]
        o = order(first)
        here = pl.ds(first, count)
        blocks = term.at[here, pl.ds(0, (16, 4, 8, 1, 2)[stage])]
        frame_copy(blocks, blocks, r_send.at[g], r_recv.at[g, stage], dev_sib).wait_recv()
        for j in range(first, first + count):
            if stage == 0:
                at = pl.ds(core_at, 16)
                term[j, at] = term[j, at] + land_a[j]
            elif stage == 1:
                there, other = pl.ds(o.col_r, 2), pl.ds(o.col_l + 2, 2)
                term[j, there] = term[j, there] + land_b1[0, j]
                term[j, other] = term[j, other] + land_b1[1, j]
            elif stage == 2:
                at = pl.ds(o.col, 4)
                term[j, at] = term[j, at] + (land_b2[0, j] + land_b2[1, j])
            elif stage == 3:
                term[j, o.own_r, 0] = term[j, o.own_r, 0] + land_c1[0, j]
                term[j, o.own_l, 1] = term[j, o.own_l, 1] + land_c1[1, j]
            else:
                grad_ref[j] = term[j, o.own] + (land_c2[0, j] + land_c2[1, j])

    def reduce_next(g, stage):
        reduce_finish(g, stage)
        reduce_start(g, stage + 1)

    def each_peer(body):
        def run(step, carry):
            body(step)
            return carry

        lax.fori_loop(1, n_chan, run, 0)

    def peers_wait(phase, blocks, sent):
        copy = chan_copy(blocks, blocks, phase, peer(1))
        if sent:
            copy.wait_send()
        else:
            copy.wait_recv()

    others = pl.ds(0, n_chan - 1)
    each_peer(lambda step: chan_copy(phases.at[me], phases.at[me], 0, peer(step)).start())
    sequence = (3, 0, 1, 2)
    for j in sequence:
        gather_start(j, 0)

    amp_copy.wait()
    scale_copy.wait()
    line = lax.broadcasted_iota(jnp.int32, (PUPIL, PUPIL), 0).astype(F32) - (PUPIL - 1) / 2.0
    column = lax.broadcasted_iota(jnp.int32, (PUPIL, PUPIL), 1).astype(F32) - (PUPIL - 1) / 2.0
    inside = line * line + column * column <= (PUPIL / 2.0) ** 2
    aperture = jnp.where(inside, amp[...], 0.0)
    total = jnp.sum(aperture * aperture, axis=(0, 1), keepdims=True)
    inverse = 1.0 / (total * float(GRID * GRID))

    for stage in (0, 1):
        for j in sequence:
            gather_next(j, stage)
    peers_wait(0, phases.at[others], False)
    tab_copy.wait()

    def table(first, count=256):
        return (
            tab[pl.ds(first, count), :].astype(BF16),
            tab[pl.ds(SECT + first, count), :].astype(BF16),
        )

    wave = phases[...].reshape(PUPIL, PUPIL)

    def fields(j, carry):
        sin_v, cos_v = sincos(scale[j] * wave)
        real, imag = aperture * cos_v, aperture * sin_v
        field[j, 0] = real
        field[j, 1] = imag
        at = pl.ds(pl.multiple_of(j * PUPIL, PUPIL), PUPIL)
        pupil[at, pl.ds(0, PUPIL)] = real
        pupil[at, pl.ds(PUPIL, PUPIL)] = imag
        return carry

    lax.fori_loop(0, channels, fields, 0)
    x_hi, x_lo = split(pupil[...])
    half[:, 0:GRID] = dot3(x_hi, x_lo, *table(T_A))
    half[:, GRID : 2 * GRID] = dot3(x_hi, x_lo, *table(T_B))

    first_lane = lax.broadcasted_iota(jnp.int32, (GRID, PUPIL), 1) == 0

    def forward(p, carry):
        density = []
        for s in range(2):
            j = 2 * p + s
            at = pl.ds(pl.multiple_of(j * PUPIL, PUPIL), PUPIL)
            r_hi, r_lo = split(half[at, 0:GRID])
            i_hi, i_lo = split(half[at, GRID : 2 * GRID])
            high = jnp.concatenate(
                [jnp.concatenate([r_hi, i_hi], 1), jnp.concatenate([i_hi, -r_hi], 1)], 0
            )
            low = jnp.concatenate(
                [jnp.concatenate([r_lo, i_lo], 1), jnp.concatenate([i_lo, -r_lo], 1)], 0
            )
            both = dot3(*table(T_L2), high, low)
            spread[j] = both
            real, imag = both[:, 0:GRID], both[:, GRID : 2 * GRID]
            density.append((real * real + imag * imag) * inverse)
        q_hi, q_lo = split(dot3(*split(jnp.concatenate(density, 0)), *table(T_H)))

        @pl.when(p == 0)
        def _():
            gather_next(0, 2)
            gather_next(3, 2)

        @pl.when(p == 1)
        def _():
            gather_next(2, 2)
            gather_next(1, 3)

        for s in range(2):
            j = 2 * p + s
            at = slice(s * GRID, (s + 1) * GRID)
            product = dot3(*table(T_C, 512), q_hi[at], q_lo[at])
            by_cos, by_sin = product[0:GRID], product[GRID : 2 * GRID]
            p1, p3 = by_cos[:, 0:PUPIL], by_cos[:, PUPIL:GRID]
            p4, p2 = by_sin[:, 0:PUPIL], by_sin[:, PUPIL:GRID]
            otf[j, :, 0:PUPIL] = p1 + jnp.where(first_lane, 0.0, p2)
            otf[j, :, GRID : GRID + PUPIL] = jnp.where(first_lane, 0.0, p3) - p4
            otf[j, :, PUPIL:GRID] = mirror(jnp.where(first_lane, p3, p1 - p2))
            otf[j, :, GRID + PUPIL : 2 * GRID] = mirror(jnp.where(first_lane, -p2, -p3 - p4))

        @pl.when(p == 0)
        def _():
            gather_next(1, 2)
            gather_next(0, 3)

        @pl.when(p == 1)
        def _():
            gather_next(3, 3)
            gather_next(2, 3)

        return carry

    lax.fori_loop(0, pairs, forward, 0)
    img_copy.wait()

    lane0 = lax.broadcasted_iota(jnp.int32, (16, PUPIL), 1) == 0

    def residual_block(p, s, b):
        j = 2 * p + s
        at = pl.ds(pl.multiple_of(b * 16, 16), 16)
        at_low = pl.ds(pl.multiple_of(b * 16 + GRID, 16), 16)
        crossed = lax.rem(b, 4) * 4 + lax.div(b, 4)
        k = jnp.where(j == last, crossed, b) if s == 1 else b
        o_r = jnp.concatenate([obj[j, k, 0], obj[j, k + 16, 0]], 0)
        o_i = jnp.concatenate([obj[j, k, 1], obj[j, k + 16, 1]], 0)
        t_r, t_i = otf[j, at, 0:GRID], otf[j, at, GRID : 2 * GRID]
        r_r = o_r * t_r - o_i * t_i - img[j, 0, 0, at, :]
        r_i = o_r * t_i + o_i * t_r - img[j, 0, 1, at, :]
        g_r = t_r * r_r + t_i * r_i
        g_i = t_r * r_i - t_i * r_r
        term[j, k, 0] = g_r[0:8]
        term[j, k + 16, 0] = g_r[8:16]
        term[j, k, 1] = g_i[0:8]
        term[j, k + 16, 1] = g_i[8:16]
        w_r = o_r * r_r + o_i * r_i
        w_i = o_r * r_i - o_i * r_r
        wr_p, wi_p = w_r[:, 0:PUPIL], w_i[:, 0:PUPIL]
        wr_m, wi_m = mirror(w_r[:, PUPIL:GRID]), mirror(w_i[:, PUPIL:GRID])
        top = jnp.concatenate(
            [wr_p + jnp.where(lane0, 0.0, wr_m), jnp.where(lane0, wr_m, wi_p - wi_m)], 1
        )
        low = jnp.concatenate(
            [-(wi_p + jnp.where(lane0, 0.0, wi_m)), jnp.where(lane0, -wi_m, wr_p - wr_m)], 1
        )
        weight[j, at, :] = top
        weight[j, at_low, :] = low

    def residual(p):
        def run(b, carry):
            for s in range(2):
                residual_block(p, s, b)
            return carry

        lax.fori_loop(0, GRID // 16, run, 0, unroll=2)

    pgrad[...] = jnp.zeros_like(pgrad)

    def way_back(p, carry):
        gather_wait(2 * p, 4)
        gather_wait(2 * p + 1, 4)
        residual(p)

        @pl.when(p == 0)
        def _():
            reduce_start(0, 0)

        @pl.when(p == 1)
        def _():
            reduce_start(1, 0)
            reduce_start(2, 0)
            reduce_next(0, 1)

        c_hi, c_lo = table(T_C)
        s_hi, s_lo = table(T_S)
        high = jnp.concatenate([c_hi, s_hi], 1)
        low = jnp.concatenate([c_lo, s_lo], 1)
        back = jnp.concatenate([dot3(high, low, *split(weight[2 * p + s])) for s in range(2)], 0)
        change = dot3(*split(back), *table(T_HT)) * (2.0 * inverse)
        for s in range(2):
            j = 2 * p + s
            at = pl.ds(s * GRID, GRID)
            here = change[s * GRID : (s + 1) * GRID]
            for part_at in (pl.ds(0, GRID), pl.ds(GRID, GRID)):
                along[p, at, part_at] = here * spread[j, :, part_at]

        @pl.when(p == 0)
        def _():
            reduce_next(0, 0)

        @pl.when(p == 1)
        def _():
            reduce_next(1, 0)
            reduce_next(2, 0)

        return carry

    lax.fori_loop(0, pairs, way_back, 0)

    def to_pupil(p, carry):
        b_hi, b_lo = split(dot3(*split(along[p]), *table(T_BACK, 512)))
        for s in range(2):
            j = 2 * p + s
            at = slice(s * GRID, (s + 1) * GRID)
            g = dot3(*table(T_A), b_hi[at], b_lo[at])
            g_r = g[0:PUPIL, 0:PUPIL] - g[PUPIL:GRID, PUPIL:GRID]
            g_i = g[PUPIL:GRID, 0:PUPIL] + g[0:PUPIL, PUPIL:GRID]
            change = scale[j] * (field[j, 0] * g_i - field[j, 1] * g_r)
            pgrad[...] = pgrad[...] + change.reshape(pgrad.shape)

        @pl.when(p == 0)
        def _():
            reduce_next(1, 1)
            reduce_next(2, 1)
            reduce_next(0, 2)

        return carry

    lax.fori_loop(0, pairs, to_pupil, 0)
    each_peer(lambda step: chan_copy(pgrad.at[peer(step)], land_pg.at[step], 1, peer(step)).start())
    reduce_next(0, 3)
    reduce_next(1, 2)
    reduce_next(2, 2)

    part[...] = jnp.zeros_like(part)
    peers_wait(1, land_pg.at[others], False)
    summed = pgrad[me]
    for step in range(1, n_chan):
        summed = summed + land_pg[step]
    for m in range(modes):
        part[m : m + 1, :] = jnp.sum(maps[m] * summed, axis=0, keepdims=True)
    vec[...] = lax.dot_general(
        jnp.ones((8, PUPIL), F32),
        part[...],
        (((1,), (1,)), ((), ())),
        precision=lax.Precision.HIGHEST,
        preferred_element_type=F32,
    )
    each_peer(lambda step: chan_copy(vec, land_vec.at[step], 2, peer(step)).start())
    reduce_next(1, 3)
    reduce_next(2, 3)
    reduce_finish(0, 4)
    peers_wait(2, land_vec.at[others], False)
    answer = vec[...]
    for step in range(1, n_chan):
        answer = answer + land_vec[step]
    mode_ref[...] = answer[0:1, 0:modes]
    reduce_finish(1, 4)
    reduce_finish(2, 4)

    for j in range(channels):
        blocks = obj.at[j, pl.ds(0, 31)]
        frame_copy(blocks, blocks, g_send.at[j], g_recv.at[j, 0], dev_sib).wait_send()
    for g, (first, count) in enumerate(groups):
        blocks = term.at[pl.ds(first, count), pl.ds(0, 31)]
        frame_copy(blocks, blocks, r_send.at[g], r_recv.at[g, 0], dev_sib).wait_send()
    peers_wait(0, phases.at[others], True)
    peers_wait(1, land_pg.at[others], True)
    peers_wait(2, land_vec.at[others], True)


def on_device(n_chan, images, objects, coeffs, mode_maps, amplitude, phase_scale):
    channels = images.shape[0]
    modes = coeffs.shape[1]
    rows = mode_maps.shape[1]
    vmem = pl.BlockSpec(memory_space=pltpu.VMEM)
    hbm = pl.BlockSpec(memory_space=pltpu.HBM)
    dma = pltpu.SemaphoreType.DMA
    block = (2, 8, GRID)
    two = channels // 2
    outs = (
        jax.ShapeDtypeStruct(objects.shape, F32),
        jax.ShapeDtypeStruct(coeffs.shape, F32),
    )
    inputs = (images, objects, coeffs, mode_maps, amplitude, phase_scale, jnp.asarray(build_tables()))
    return pl.pallas_call(
        functools.partial(kernel, n_chan, channels, modes),
        out_shape=outs,
        in_specs=[hbm] * 7,
        out_specs=(vmem, vmem),
        scratch_shapes=[
            pltpu.SMEM(coeffs.shape, F32),
            pltpu.SMEM(phase_scale.shape, F32),
            pltpu.VMEM(mode_maps.shape, F32),
            pltpu.VMEM(amplitude.shape, F32),
            pltpu.VMEM(images.shape, F32),
            pltpu.VMEM((2 * SECT, GRID), F32),
            pltpu.VMEM((channels, 32) + block, F32),
            pltpu.VMEM((channels, 32) + block, F32),
            pltpu.VMEM((channels, 16) + block, F32),
            pltpu.VMEM((2, channels, 2) + block, F32),
            pltpu.VMEM((2, channels, 4) + block, F32),
            pltpu.VMEM((2, channels, 8, GRID), F32),
            pltpu.VMEM((2, channels) + block, F32),
            pltpu.VMEM((n_chan, rows, PUPIL), F32),
            pltpu.VMEM((channels, 2, PUPIL, PUPIL), F32),
            pltpu.VMEM((channels * PUPIL, GRID), F32),
            pltpu.VMEM((channels * PUPIL, 2 * GRID), F32),
            pltpu.VMEM((channels, GRID, 2 * GRID), F32),
            pltpu.VMEM((channels, GRID, 2 * GRID), F32),
            pltpu.VMEM((channels, 2 * GRID, GRID), F32),
            pltpu.VMEM((two, 2 * GRID, 2 * GRID), F32),
            pltpu.VMEM((n_chan, rows, PUPIL), F32),
            pltpu.VMEM((n_chan, rows, PUPIL), F32),
            pltpu.VMEM((PUPIL, PUPIL), F32),
            pltpu.VMEM((8, PUPIL), F32),
            pltpu.VMEM((n_chan, 8, PUPIL), F32),
            dma((8,)),
            dma((3,)),
            dma((3,)),
            dma((channels,)),
            dma((channels, 5)),
            dma((3,)),
            dma((3, 5)),
        ],
        compiler_params=pltpu.CompilerParams(
            collective_id=0, has_side_effects=True, vmem_limit_bytes=48 * 1024 * 1024
        ),
        name="deconvolve",
    )(*[pltpu.with_memory_space_constraint(value, pltpu.HBM) for value in inputs])


def solution(mesh):
    return jax.shard_map(
        functools.partial(on_device, mesh.shape["chan"]),
        mesh=mesh,
        in_specs=(
            P("chan", "frame", None, None, None),
            P("chan", None, "frame", None),
            P("frame", None),
            P(None, "chan", None),
            P(),
            P("chan"),
        ),
        out_specs=(P("chan", None, "frame", None), P("frame", None)),
        check_vma=False,
    )
```

```python
import functools
import math

import jax
import jax.numpy as jnp
import ml_dtypes
import numpy as np
from jax import lax
from jax.experimental import pallas as pl
from jax.experimental.pallas import tpu as pltpu
from jax.sharding import PartitionSpec as P

F32 = jnp.float32
BF16 = jnp.bfloat16
MESH = pl.DeviceIdType.MESH
GRID = 256
PUPIL = 128
SECT = 2304

T_A, T_B, T_L2, T_H, T_C, T_S, T_HT, T_BACK = 0, 256, 512, 768, 1024, 1280, 1536, 1792


def build_tables():
    index = np.arange(GRID)
    turn = (np.outer(index, index) % GRID) * (2.0 * math.pi / GRID)
    cos, sin = np.cos(turn), np.sin(turn)
    half = PUPIL
    first = np.concatenate([cos[:half], sin[:half]], 0)
    second = np.concatenate([-sin[:half], cos[:half]], 0)
    left = np.concatenate([cos[:, :half], sin[:, :half]], 1)
    minus = -sin[:, :half]
    minus[:, 0] = cos[:, half]
    herm = np.concatenate([cos[:, :half], minus], 1)
    back = np.concatenate(
        [
            np.concatenate([cos[:, :half], sin[:, :half]], 1),
            np.concatenate([-sin[:, :half], cos[:, :half]], 1),
        ],
        0,
    )
    table = np.concatenate([first, second, left, herm, cos, sin, herm.T, back], 0).astype(np.float32)
    high = table.astype(ml_dtypes.bfloat16)
    high = high.astype(np.float32)
    low = (table - high).astype(ml_dtypes.bfloat16).astype(np.float32)
    return np.concatenate([high, low], 0)


def split(value):
    high = value.astype(BF16)
    low = (value - high.astype(F32)).astype(BF16)
    return high, low


def dot(a, b):
    return jnp.dot(a, b, preferred_element_type=F32)


def dot3(a_high, a_low, b_high, b_low):
    left = jnp.concatenate([a_high, a_low, a_high], 1)
    right = jnp.concatenate([b_high, b_high, b_low], 0)
    return dot(left, right)


def sincos(angle):
    k = jnp.floor(angle * (2.0 / math.pi) + 0.5)
    r = ((angle - k * 1.5703125) - k * 4.837512969970703125e-4) - k * 7.54978995489188216e-8
    z = r * r
    sin_r = ((-1.9515295891e-4 * z + 8.3321608736e-3) * z - 1.6666654611e-1) * z * r + r
    cos_r = ((2.443315711809948e-5 * z - 1.388731625493765e-3) * z + 4.166664568298827e-2) * z * z - 0.5 * z + 1.0
    quad = k - 4.0 * jnp.floor(k * 0.25)
    odd = (quad == 1.0) | (quad == 3.0)
    sin_v = jnp.where(odd, cos_r, sin_r)
    cos_v = jnp.where(odd, sin_r, cos_r)
    sin_v = jnp.where(quad >= 2.0, -sin_v, sin_v)
    cos_v = jnp.where((quad == 1.0) | (quad == 2.0), -cos_v, cos_v)
    return sin_v, cos_v


def mirror(value):
    lane = lax.broadcasted_iota(jnp.int32, value.shape, 1)
    index = (PUPIL - lane) & (PUPIL - 1)
    return jnp.take_along_axis(value, index, axis=1, mode="promise_in_bounds")


def kernel(
    n_chan,
    channels,
    modes,
    images_hbm,
    objects_hbm,
    coeffs_hbm,
    maps_hbm,
    amp_hbm,
    scale_hbm,
    table_hbm,
    grad_ref,
    mode_ref,
    coeffs,
    scale,
    maps,
    amp,
    img,
    tab,
    obj,
    term,
    land_a,
    land_b1,
    land_b2,
    land_c1,
    land_c2,
    phases,
    field,
    pupil,
    half,
    spread,
    otf,
    weight,
    along,
    pgrad,
    land_pg,
    part,
    vec,
    land_vec,
    local_sem,
    peer_send,
    peer_recv,
    g_send,
    g_recv,
    r_send,
    r_recv,
):
    pairs = channels // 2
    me = lax.axis_index("chan")
    fr = lax.axis_index("frame")
    cx = lax.div(fr, 8)
    cy = lax.rem(lax.div(fr, 2), 4)
    cc = lax.rem(fr, 2)
    x_r, x_l = lax.rem(cx + 1, 4), lax.rem(cx + 3, 4)
    y_r, y_l = lax.rem(cy + 1, 4), lax.rem(cy + 3, 4)
    sib = 1 - cc
    dev_xr = x_r * 8 + cy * 2 + cc
    dev_xl = x_l * 8 + cy * 2 + cc
    dev_yr = cx * 8 + y_r * 2 + cc
    dev_yl = cx * 8 + y_l * 2 + cc
    dev_xo = lax.rem(cx + 2, 4) * 8 + cy * 2 + cc
    dev_yo = cx * 8 + lax.rem(cy + 2, 4) * 2 + cc
    dev_sib = cx * 8 + cy * 2 + sib
    core_at = cc * 16
    sib_at = sib * 16

    class Order:
        def __init__(self, major, minor, devices):
            self.col, self.col_r, self.col_l, self.col_o = [
                core_at + lax.rem(major + step, 4) * 4 for step in (0, 1, 3, 2)
            ]
            self.own, self.own_r, self.own_l, self.own_o = [
                self.col + lax.rem(minor + step, 4) for step in (0, 1, 3, 2)
            ]
            self.major_r, self.major_l, self.minor_r, self.minor_l, self.minor_o = devices

    by_column = Order(cx, cy, (dev_xr, dev_xl, dev_yr, dev_yl, dev_yo))
    by_row = Order(cy, cx, (dev_yr, dev_yl, dev_xr, dev_xl, dev_xo))
    last = channels - 1

    def order(j):
        return by_row if j == last else by_column

    def peer(step):
        return lax.rem(me + step, n_chan)

    def local(k, src, dst):
        copy = pltpu.make_async_copy(src, dst, local_sem.at[k])
        copy.start()
        return copy

    maps_copy = local(0, maps_hbm, maps)
    coeffs_copy = local(1, coeffs_hbm, coeffs)
    obj_copies = [
        local(2, objects_hbm.at[pl.ds(0, last)], obj.at[pl.ds(0, last), by_column.own]),
        local(7, objects_hbm.at[last], obj.at[last, by_row.own]),
    ]
    scale_copy = local(3, scale_hbm, scale)
    amp_copy = local(4, amp_hbm, amp)
    tab_copy = local(5, table_hbm, tab)
    img_copy = local(6, images_hbm, img)
    barrier = pltpu.get_barrier_semaphore()
    for dev in (dev_yr, dev_yl, dev_yo, dev_xr, dev_xl, dev_xo, dev_sib):
        pl.semaphore_signal(barrier, inc=1, device_id={"frame": dev}, device_id_type=MESH)
    for step in range(1, n_chan):
        pl.semaphore_signal(barrier, inc=1, device_id={"chan": peer(step)}, device_id_type=MESH)

    maps_copy.wait()
    coeffs_copy.wait()
    mine = coeffs[0, 0] * maps[0]
    for m in range(1, modes):
        mine = mine + coeffs[0, m] * maps[m]
    phases[me] = mine
    for copy in obj_copies:
        copy.wait()
    pl.semaphore_wait(barrier, 7 + n_chan - 1)

    def frame_copy(src, dst, send, recv, dev):
        return pltpu.make_async_remote_copy(
            src_ref=src,
            dst_ref=dst,
            send_sem=send,
            recv_sem=recv,
            device_id={"frame": dev},
            device_id_type=MESH,
        )

    def chan_copy(src, dst, phase, dev):
        return pltpu.make_async_remote_copy(
            src_ref=src,
            dst_ref=dst,
            send_sem=peer_send.at[phase],
            recv_sem=peer_recv.at[phase],
            device_id={"chan": dev},
            device_id_type=MESH,
        )

    at_once = (0,)
    groups_at_once = (1, 2)

    def gather_start(j, stage):
        o = order(j)
        across = []
        if stage == 0:
            sent = [(obj.at[j, o.own], o.minor_r), (obj.at[j, o.own], o.minor_l)]
            if j in at_once:
                sent.append((obj.at[j, o.own], o.minor_o))
        elif stage == 1:
            sent = [(obj.at[j, o.own_l, 0], o.minor_r), (obj.at[j, o.own_r, 1], o.minor_l)]
        elif stage == 2:
            sent = [(obj.at[j, pl.ds(o.col, 4)], o.major_r), (obj.at[j, pl.ds(o.col, 4)], o.major_l)]
            across = [o.col]
        elif stage == 3:
            sent = [
                (obj.at[j, pl.ds(o.col_l, 2)], o.major_r),
                (obj.at[j, pl.ds(o.col_r + 2, 2)], o.major_l),
            ]
            across = [o.col_r, o.col_l]
        else:
            sent = []
            across = [o.col_o]
        for src, dev in sent:
            frame_copy(src, src, g_send.at[j], g_recv.at[j, stage], dev).start()
        for col in across:
            src = obj.at[j, pl.ds(col, 4)]
            frame_copy(src, src, g_send.at[j], g_recv.at[j, 4], dev_sib).start()

    def gather_wait(j, stage):
        direct = stage == 0 and not isinstance(j, jax.Array) and j in at_once
        blocks = obj.at[j, pl.ds(0, 3 if direct else (2, 1, 8, 4, 16)[stage])]
        frame_copy(blocks, blocks, g_send.at[j], g_recv.at[j, stage], dev_sib).wait_recv()

    def gather_next(j, stage):
        gather_wait(j, stage)
        gather_start(j, 2 if stage == 0 and j in at_once else stage + 1)

    groups = ((0, 2), (2, 1), (3, 1))

    def reduce_start(g, stage):
        first, count = groups[g]
        o = order(first)
        here = pl.ds(first, count)
        if stage == 0:
            sent = [
                (term.at[here, pl.ds(sib_at + col, 4)], land_a.at[here, pl.ds(col, 4)], dev_sib)
                for col in [at - core_at for at in (o.col_o, o.col_r, o.col_l, o.col)]
            ]
        elif stage == 1:
            sent = [
                (term.at[here, pl.ds(o.col_o, 2)], land_b1.at[0, here], o.major_r),
                (term.at[here, pl.ds(o.col_o + 2, 2)], land_b1.at[1, here], o.major_l),
            ]
        elif stage == 2:
            sent = [
                (term.at[here, pl.ds(o.col_r, 4)], land_b2.at[0, here], o.major_r),
                (term.at[here, pl.ds(o.col_l, 4)], land_b2.at[1, here], o.major_l),
            ]
        elif stage == 3:
            sent = [
                (term.at[here, o.own_o, 0], land_c1.at[0, here], o.minor_r),
                (term.at[here, o.own_o, 1], land_c1.at[1, here], o.minor_l),
            ]
        else:
            sent = [
                (term.at[here, o.own_r], land_c2.at[0, here], o.minor_r),
                (term.at[here, o.own_l], land_c2.at[1, here], o.minor_l),
            ]
            if g in groups_at_once:
                sent.append((term.at[here, o.own_o], land_c2.at[2, here], o.minor_o))
        for src, land, dev in sent:
            frame_copy(src, land, r_send.at[g], r_recv.at[g, stage], dev).start()

    def reduce_finish(g, stage):
        first, count = groups[g]
        o = order(first)
        here = pl.ds(first, count)
        direct = g in groups_at_once
        blocks = term.at[here, pl.ds(0, (16, 4, 8, 1, 3 if direct else 2)[stage])]
        frame_copy(blocks, blocks, r_send.at[g], r_recv.at[g, stage], dev_sib).wait_recv()
        for j in range(first, first + count):
            if stage == 0:
                at = pl.ds(core_at, 16)
                term[j, at] = term[j, at] + land_a[j]
            elif stage == 1:
                there, other = pl.ds(o.col_r, 2), pl.ds(o.col_l + 2, 2)
                term[j, there] = term[j, there] + land_b1[0, j]
                term[j, other] = term[j, other] + land_b1[1, j]
            elif stage == 2:
                at = pl.ds(o.col, 4)
                term[j, at] = term[j, at] + (land_b2[0, j] + land_b2[1, j])
            elif stage == 3:
                term[j, o.own_r, 0] = term[j, o.own_r, 0] + land_c1[0, j]
                term[j, o.own_l, 1] = term[j, o.own_l, 1] + land_c1[1, j]
            else:
                landed = land_c2[0, j] + land_c2[1, j]
                if direct:
                    landed = landed + land_c2[2, j]
                grad_ref[j] = term[j, o.own] + landed

    def reduce_next(g, stage):
        reduce_finish(g, stage)
        reduce_start(g, 4 if stage == 2 and g in groups_at_once else stage + 1)

    def each_peer(body):
        def run(step, carry):
            body(step)
            return carry

        lax.fori_loop(1, n_chan, run, 0)

    def peers_wait(phase, blocks, sent):
        copy = chan_copy(blocks, blocks, phase, peer(1))
        if sent:
            copy.wait_send()
        else:
            copy.wait_recv()

    others = pl.ds(0, n_chan - 1)
    each_peer(lambda step: chan_copy(phases.at[me], phases.at[me], 0, peer(step)).start())
    sequence = (0, 3, 1, 2)
    for j in sequence:
        gather_start(j, 0)

    amp_copy.wait()
    scale_copy.wait()
    line = lax.broadcasted_iota(jnp.int32, (PUPIL, PUPIL), 0).astype(F32) - (PUPIL - 1) / 2.0
    column = lax.broadcasted_iota(jnp.int32, (PUPIL, PUPIL), 1).astype(F32) - (PUPIL - 1) / 2.0
    inside = line * line + column * column <= (PUPIL / 2.0) ** 2
    aperture = jnp.where(inside, amp[...], 0.0)
    total = jnp.sum(aperture * aperture, axis=(0, 1), keepdims=True)
    inverse = 1.0 / (total * float(GRID * GRID))

    for stage in (0, 1):
        for j in sequence:
            if not (stage == 1 and j in at_once):
                gather_next(j, stage)
    peers_wait(0, phases.at[others], False)
    tab_copy.wait()

    def table(first, count=256):
        return (
            tab[pl.ds(first, count), :].astype(BF16),
            tab[pl.ds(SECT + first, count), :].astype(BF16),
        )

    wave = phases[...].reshape(PUPIL, PUPIL)

    def fields(j, carry):
        sin_v, cos_v = sincos(scale[j] * wave)
        real, imag = aperture * cos_v, aperture * sin_v
        field[j, 0] = real
        field[j, 1] = imag
        at = pl.ds(pl.multiple_of(j * PUPIL, PUPIL), PUPIL)
        pupil[at, pl.ds(0, PUPIL)] = real
        pupil[at, pl.ds(PUPIL, PUPIL)] = imag
        return carry

    lax.fori_loop(0, channels, fields, 0)
    x_hi, x_lo = split(pupil[...])
    half[:, 0:GRID] = dot3(x_hi, x_lo, *table(T_A))
    half[:, GRID : 2 * GRID] = dot3(x_hi, x_lo, *table(T_B))

    first_lane = lax.broadcasted_iota(jnp.int32, (GRID, PUPIL), 1) == 0

    def forward(p, carry):
        density = []
        for s in range(2):
            j = 2 * p + s
            at = pl.ds(pl.multiple_of(j * PUPIL, PUPIL), PUPIL)
            r_hi, r_lo = split(half[at, 0:GRID])
            i_hi, i_lo = split(half[at, GRID : 2 * GRID])
            high = jnp.concatenate(
                [jnp.concatenate([r_hi, i_hi], 1), jnp.concatenate([i_hi, -r_hi], 1)], 0
            )
            low = jnp.concatenate(
                [jnp.concatenate([r_lo, i_lo], 1), jnp.concatenate([i_lo, -r_lo], 1)], 0
            )
            both = dot3(*table(T_L2), high, low)
            spread[j] = both
            real, imag = both[:, 0:GRID], both[:, GRID : 2 * GRID]
            density.append((real * real + imag * imag) * inverse)
        q_hi, q_lo = split(dot3(*split(jnp.concatenate(density, 0)), *table(T_H)))

        @pl.when(p == 0)
        def _():
            gather_next(0, 2)
            gather_next(3, 2)

        @pl.when(p == 1)
        def _():
            gather_next(2, 2)
            gather_next(1, 3)

        for s in range(2):
            j = 2 * p + s
            at = slice(s * GRID, (s + 1) * GRID)
            product = dot3(*table(T_C, 512), q_hi[at], q_lo[at])
            by_cos, by_sin = product[0:GRID], product[GRID : 2 * GRID]
            p1, p3 = by_cos[:, 0:PUPIL], by_cos[:, PUPIL:GRID]
            p4, p2 = by_sin[:, 0:PUPIL], by_sin[:, PUPIL:GRID]
            otf[j, :, 0:PUPIL] = p1 + jnp.where(first_lane, 0.0, p2)
            otf[j, :, GRID : GRID + PUPIL] = jnp.where(first_lane, 0.0, p3) - p4
            otf[j, :, PUPIL:GRID] = mirror(jnp.where(first_lane, p3, p1 - p2))
            otf[j, :, GRID + PUPIL : 2 * GRID] = mirror(jnp.where(first_lane, -p2, -p3 - p4))

        @pl.when(p == 0)
        def _():
            gather_next(1, 2)
            gather_next(0, 3)

        @pl.when(p == 1)
        def _():
            gather_next(3, 3)
            gather_next(2, 3)

        return carry

    lax.fori_loop(0, pairs, forward, 0)
    img_copy.wait()

    lane0 = lax.broadcasted_iota(jnp.int32, (16, PUPIL), 1) == 0

    def residual_block(p, s, b):
        j = 2 * p + s
        at = pl.ds(pl.multiple_of(b * 16, 16), 16)
        at_low = pl.ds(pl.multiple_of(b * 16 + GRID, 16), 16)
        crossed = lax.rem(b, 4) * 4 + lax.div(b, 4)
        k = jnp.where(j == last, crossed, b) if s == 1 else b
        o_r = jnp.concatenate([obj[j, k, 0], obj[j, k + 16, 0]], 0)
        o_i = jnp.concatenate([obj[j, k, 1], obj[j, k + 16, 1]], 0)
        t_r, t_i = otf[j, at, 0:GRID], otf[j, at, GRID : 2 * GRID]
        r_r = o_r * t_r - o_i * t_i - img[j, 0, 0, at, :]
        r_i = o_r * t_i + o_i * t_r - img[j, 0, 1, at, :]
        g_r = t_r * r_r + t_i * r_i
        g_i = t_r * r_i - t_i * r_r
        term[j, k, 0] = g_r[0:8]
        term[j, k + 16, 0] = g_r[8:16]
        term[j, k, 1] = g_i[0:8]
        term[j, k + 16, 1] = g_i[8:16]
        w_r = o_r * r_r + o_i * r_i
        w_i = o_r * r_i - o_i * r_r
        wr_p, wi_p = w_r[:, 0:PUPIL], w_i[:, 0:PUPIL]
        wr_m, wi_m = mirror(w_r[:, PUPIL:GRID]), mirror(w_i[:, PUPIL:GRID])
        top = jnp.concatenate(
            [wr_p + jnp.where(lane0, 0.0, wr_m), jnp.where(lane0, wr_m, wi_p - wi_m)], 1
        )
        low = jnp.concatenate(
            [-(wi_p + jnp.where(lane0, 0.0, wi_m)), jnp.where(lane0, -wi_m, wr_p - wr_m)], 1
        )
        weight[j, at, :] = top
        weight[j, at_low, :] = low

    def residual(p):
        def run(b, carry):
            for s in range(2):
                residual_block(p, s, b)
            return carry

        lax.fori_loop(0, GRID // 16, run, 0, unroll=2)

    pgrad[...] = jnp.zeros_like(pgrad)

    def way_back(p, carry):
        gather_wait(2 * p, 4)
        gather_wait(2 * p + 1, 4)
        residual(p)

        @pl.when(p == 0)
        def _():
            reduce_start(0, 0)

        @pl.when(p == 1)
        def _():
            reduce_start(1, 0)
            reduce_start(2, 0)
            reduce_next(0, 1)

        c_hi, c_lo = table(T_C)
        s_hi, s_lo = table(T_S)
        high = jnp.concatenate([c_hi, s_hi], 1)
        low = jnp.concatenate([c_lo, s_lo], 1)
        back = jnp.concatenate([dot3(high, low, *split(weight[2 * p + s])) for s in range(2)], 0)
        change = dot3(*split(back), *table(T_HT)) * (2.0 * inverse)
        for s in range(2):
            j = 2 * p + s
            at = pl.ds(s * GRID, GRID)
            here = change[s * GRID : (s + 1) * GRID]
            for part_at in (pl.ds(0, GRID), pl.ds(GRID, GRID)):
                along[p, at, part_at] = here * spread[j, :, part_at]

        @pl.when(p == 0)
        def _():
            reduce_next(0, 0)

        @pl.when(p == 1)
        def _():
            reduce_next(1, 0)
            reduce_next(2, 0)

        return carry

    lax.fori_loop(0, pairs, way_back, 0)

    def to_pupil(p, carry):
        b_hi, b_lo = split(dot3(*split(along[p]), *table(T_BACK, 512)))
        for s in range(2):
            j = 2 * p + s
            at = slice(s * GRID, (s + 1) * GRID)
            g = dot3(*table(T_A), b_hi[at], b_lo[at])
            g_r = g[0:PUPIL, 0:PUPIL] - g[PUPIL:GRID, PUPIL:GRID]
            g_i = g[PUPIL:GRID, 0:PUPIL] + g[0:PUPIL, PUPIL:GRID]
            change = scale[j] * (field[j, 0] * g_i - field[j, 1] * g_r)
            pgrad[...] = pgrad[...] + change.reshape(pgrad.shape)

        @pl.when(p == 0)
        def _():
            reduce_next(1, 1)
            reduce_next(2, 1)
            reduce_next(0, 2)

        return carry

    lax.fori_loop(0, pairs, to_pupil, 0)
    each_peer(lambda step: chan_copy(pgrad.at[peer(step)], land_pg.at[step], 1, peer(step)).start())
    reduce_next(0, 3)
    reduce_next(1, 2)
    reduce_next(2, 2)

    part[...] = jnp.zeros_like(part)
    peers_wait(1, land_pg.at[others], False)
    summed = pgrad[me]
    for step in range(1, n_chan):
        summed = summed + land_pg[step]
    for m in range(modes):
        part[m : m + 1, :] = jnp.sum(maps[m] * summed, axis=0, keepdims=True)
    vec[...] = lax.dot_general(
        jnp.ones((8, PUPIL), F32),
        part[...],
        (((1,), (1,)), ((), ())),
        precision=lax.Precision.HIGHEST,
        preferred_element_type=F32,
    )
    each_peer(lambda step: chan_copy(vec, land_vec.at[step], 2, peer(step)).start())
    reduce_finish(0, 4)
    peers_wait(2, land_vec.at[others], False)
    answer = vec[...]
    for step in range(1, n_chan):
        answer = answer + land_vec[step]
    mode_ref[...] = answer[0:1, 0:modes]
    reduce_finish(1, 4)
    reduce_finish(2, 4)

    for j in range(channels):
        blocks = obj.at[j, pl.ds(0, 31)]
        frame_copy(blocks, blocks, g_send.at[j], g_recv.at[j, 0], dev_sib).wait_send()
    for g, (first, count) in enumerate(groups):
        blocks = term.at[pl.ds(first, count), pl.ds(0, 31)]
        frame_copy(blocks, blocks, r_send.at[g], r_recv.at[g, 0], dev_sib).wait_send()
    peers_wait(0, phases.at[others], True)
    peers_wait(1, land_pg.at[others], True)
    peers_wait(2, land_vec.at[others], True)


def on_device(n_chan, images, objects, coeffs, mode_maps, amplitude, phase_scale):
    channels = images.shape[0]
    modes = coeffs.shape[1]
    rows = mode_maps.shape[1]
    vmem = pl.BlockSpec(memory_space=pltpu.VMEM)
    hbm = pl.BlockSpec(memory_space=pltpu.HBM)
    dma = pltpu.SemaphoreType.DMA
    block = (2, 8, GRID)
    two = channels // 2
    outs = (
        jax.ShapeDtypeStruct(objects.shape, F32),
        jax.ShapeDtypeStruct(coeffs.shape, F32),
    )
    inputs = (images, objects, coeffs, mode_maps, amplitude, phase_scale, jnp.asarray(build_tables()))
    return pl.pallas_call(
        functools.partial(kernel, n_chan, channels, modes),
        out_shape=outs,
        in_specs=[hbm] * 7,
        out_specs=(vmem, vmem),
        scratch_shapes=[
            pltpu.SMEM(coeffs.shape, F32),
            pltpu.SMEM(phase_scale.shape, F32),
            pltpu.VMEM(mode_maps.shape, F32),
            pltpu.VMEM(amplitude.shape, F32),
            pltpu.VMEM(images.shape, F32),
            pltpu.VMEM((2 * SECT, GRID), F32),
            pltpu.VMEM((channels, 32) + block, F32),
            pltpu.VMEM((channels, 32) + block, F32),
            pltpu.VMEM((channels, 16) + block, F32),
            pltpu.VMEM((2, channels, 2) + block, F32),
            pltpu.VMEM((2, channels, 4) + block, F32),
            pltpu.VMEM((2, channels, 8, GRID), F32),
            pltpu.VMEM((3, channels) + block, F32),
            pltpu.VMEM((n_chan, rows, PUPIL), F32),
            pltpu.VMEM((channels, 2, PUPIL, PUPIL), F32),
            pltpu.VMEM((channels * PUPIL, GRID), F32),
            pltpu.VMEM((channels * PUPIL, 2 * GRID), F32),
            pltpu.VMEM((channels, GRID, 2 * GRID), F32),
            pltpu.VMEM((channels, GRID, 2 * GRID), F32),
            pltpu.VMEM((channels, 2 * GRID, GRID), F32),
            pltpu.VMEM((two, 2 * GRID, 2 * GRID), F32),
            pltpu.VMEM((n_chan, rows, PUPIL), F32),
            pltpu.VMEM((n_chan, rows, PUPIL), F32),
            pltpu.VMEM((PUPIL, PUPIL), F32),
            pltpu.VMEM((8, PUPIL), F32),
            pltpu.VMEM((n_chan, 8, PUPIL), F32),
            dma((8,)),
            dma((3,)),
            dma((3,)),
            dma((channels,)),
            dma((channels, 5)),
            dma((3,)),
            dma((3, 5)),
        ],
        compiler_params=pltpu.CompilerParams(
            collective_id=0, has_side_effects=True, vmem_limit_bytes=48 * 1024 * 1024
        ),
        name="deconvolve",
    )(*[pltpu.with_memory_space_constraint(value, pltpu.HBM) for value in inputs])


def solution(mesh):
    return jax.shard_map(
        functools.partial(on_device, mesh.shape["chan"]),
        mesh=mesh,
        in_specs=(
            P("chan", "frame", None, None, None),
            P("chan", None, "frame", None),
            P("frame", None),
            P(None, "chan", None),
            P(),
            P("chan"),
        ),
        out_specs=(P("chan", None, "frame", None), P("frame", None)),
        check_vma=False,
    )
```

```python
import functools
import math

import jax
import jax.numpy as jnp
import ml_dtypes
import numpy as np
from jax import lax
from jax.experimental import pallas as pl
from jax.experimental.pallas import tpu as pltpu
from jax.sharding import PartitionSpec as P

F32 = jnp.float32
BF16 = jnp.bfloat16
MESH = pl.DeviceIdType.MESH
GRID = 256
PUPIL = 128

T_A, T_B, T_L2, T_H, T_C, T_S, T_HT, T_BACK = 0, 1, 2, 3, 4, 5, 6, 7


def build_tables():
    index = np.arange(GRID)
    turn = (np.outer(index, index) % GRID) * (2.0 * math.pi / GRID)
    cos, sin = np.cos(turn), np.sin(turn)
    half = PUPIL
    first = np.concatenate([cos[:half], sin[:half]], 0)
    second = np.concatenate([-sin[:half], cos[:half]], 0)
    left = np.concatenate([cos[:, :half], sin[:, :half]], 1)
    minus = -sin[:, :half]
    minus[:, 0] = cos[:, half]
    herm = np.concatenate([cos[:, :half], minus], 1)
    back = np.concatenate(
        [
            np.concatenate([cos[:, :half], sin[:, :half]], 1),
            np.concatenate([-sin[:, :half], cos[:, :half]], 1),
        ],
        0,
    )
    table = np.concatenate([first, second, left, herm, cos, sin, herm.T, back], 0).astype(np.float32)
    high = table.astype(ml_dtypes.bfloat16)
    high = high.astype(np.float32)
    low = (table - high).astype(ml_dtypes.bfloat16).astype(np.float32)
    return np.stack([high, low]).reshape(2, -1, GRID, GRID)


def split(value):
    high = value.astype(BF16)
    low = (value - high.astype(F32)).astype(BF16)
    return high, low


def dot(a, b):
    return jnp.dot(a, b, preferred_element_type=F32)


def dot3(a_high, a_low, b_high, b_low):
    left = jnp.concatenate([a_high, a_low, a_high], 1)
    right = jnp.concatenate([b_high, b_high, b_low], 0)
    return dot(left, right)


def sincos(angle):
    k = jnp.floor(angle * (2.0 / math.pi) + 0.5)
    r = ((angle - k * 1.5703125) - k * 4.837512969970703125e-4) - k * 7.54978995489188216e-8
    z = r * r
    sin_r = ((-1.9515295891e-4 * z + 8.3321608736e-3) * z - 1.6666654611e-1) * z * r + r
    cos_r = ((2.443315711809948e-5 * z - 1.388731625493765e-3) * z + 4.166664568298827e-2) * z * z - 0.5 * z + 1.0
    quad = k - 4.0 * jnp.floor(k * 0.25)
    odd = (quad == 1.0) | (quad == 3.0)
    sin_v = jnp.where(odd, cos_r, sin_r)
    cos_v = jnp.where(odd, sin_r, cos_r)
    sin_v = jnp.where(quad >= 2.0, -sin_v, sin_v)
    cos_v = jnp.where((quad == 1.0) | (quad == 2.0), -cos_v, cos_v)
    return sin_v, cos_v


def mirror(value):
    lane = lax.broadcasted_iota(jnp.int32, value.shape, 1)
    index = (PUPIL - lane) & (PUPIL - 1)
    return jnp.take_along_axis(value, index, axis=1, mode="promise_in_bounds")


def kernel(
    n_chan,
    channels,
    modes,
    images_hbm,
    objects_hbm,
    coeffs_hbm,
    maps_hbm,
    amp_hbm,
    scale_hbm,
    table_hbm,
    grad_ref,
    mode_ref,
    coeffs,
    scale,
    maps,
    amp,
    img,
    tab,
    obj,
    term,
    land_a,
    land_b1,
    land_b2,
    land_c1,
    land_c2,
    phases,
    pupil,
    half,
    spread,
    folded,
    product,
    weight,
    back,
    along,
    last_rows,
    pgrad,
    land_pg,
    part,
    vec,
    land_vec,
    local_sem,
    peer_send,
    peer_recv,
    g_send,
    g_recv,
    r_send,
    r_recv,
):
    pairs = channels // 2
    me = lax.axis_index("chan")
    fr = lax.axis_index("frame")
    cx = lax.div(fr, 8)
    cy = lax.rem(lax.div(fr, 2), 4)
    cc = lax.rem(fr, 2)
    x_r, x_l = lax.rem(cx + 1, 4), lax.rem(cx + 3, 4)
    y_r, y_l = lax.rem(cy + 1, 4), lax.rem(cy + 3, 4)
    sib = 1 - cc
    dev_xr = x_r * 8 + cy * 2 + cc
    dev_xl = x_l * 8 + cy * 2 + cc
    dev_yr = cx * 8 + y_r * 2 + cc
    dev_yl = cx * 8 + y_l * 2 + cc
    dev_sib = cx * 8 + cy * 2 + sib
    core_at = cc * 16
    sib_at = sib * 16

    class Order:
        def __init__(self, major, minor, devices):
            self.col, self.col_r, self.col_l, self.col_o = [
                core_at + lax.rem(major + step, 4) * 4 for step in (0, 1, 3, 2)
            ]
            self.own, self.own_r, self.own_l, self.own_o = [
                self.col + lax.rem(minor + step, 4) for step in (0, 1, 3, 2)
            ]
            self.major_r, self.major_l, self.minor_r, self.minor_l = devices

    by_column = Order(cx, cy, (dev_xr, dev_xl, dev_yr, dev_yl))
    by_row = Order(cy, cx, (dev_yr, dev_yl, dev_xr, dev_xl))
    last = channels - 1

    def order(j):
        return by_row if j == last else by_column

    def peer(step):
        return lax.rem(me + step, n_chan)

    def local(k, src, dst):
        copy = pltpu.make_async_copy(src, dst, local_sem.at[k])
        copy.start()
        return copy

    maps_copy = local(0, maps_hbm, maps)
    coeffs_copy = local(1, coeffs_hbm, coeffs)
    obj_copies = [
        local(2, objects_hbm.at[pl.ds(0, last)], obj.at[pl.ds(0, last), by_column.own]),
        local(7, objects_hbm.at[last], obj.at[last, by_row.own]),
    ]
    scale_copy = local(3, scale_hbm, scale)
    amp_copy = local(4, amp_hbm, amp)
    tab_copy = local(5, table_hbm, tab)
    img_copy = local(6, images_hbm, img)
    barrier = pltpu.get_barrier_semaphore()
    for dev in (dev_yr, dev_yl, dev_xr, dev_xl, dev_sib):
        pl.semaphore_signal(barrier, inc=1, device_id={"frame": dev}, device_id_type=MESH)
    for step in range(1, n_chan):
        pl.semaphore_signal(barrier, inc=1, device_id={"chan": peer(step)}, device_id_type=MESH)

    maps_copy.wait()
    coeffs_copy.wait()
    mine = coeffs[0, 0] * maps[0]
    for m in range(1, modes):
        mine = mine + coeffs[0, m] * maps[m]
    phases[me] = mine
    for copy in obj_copies:
        copy.wait()
    pl.semaphore_wait(barrier, 5 + n_chan - 1)

    def frame_copy(src, dst, send, recv, dev):
        return pltpu.make_async_remote_copy(
            src_ref=src,
            dst_ref=dst,
            send_sem=send,
            recv_sem=recv,
            device_id={"frame": dev},
            device_id_type=MESH,
        )

    def chan_copy(src, dst, phase, dev):
        return pltpu.make_async_remote_copy(
            src_ref=src,
            dst_ref=dst,
            send_sem=peer_send.at[phase],
            recv_sem=peer_recv.at[phase],
            device_id={"chan": dev},
            device_id_type=MESH,
        )

    def gather_start(j, stage):
        o = order(j)
        across = []
        if stage == 0:
            sent = [(obj.at[j, o.own], o.minor_r), (obj.at[j, o.own], o.minor_l)]
        elif stage == 1:
            sent = [(obj.at[j, o.own_l, 0], o.minor_r), (obj.at[j, o.own_r, 1], o.minor_l)]
        elif stage == 2:
            sent = [(obj.at[j, pl.ds(o.col, 4)], o.major_r), (obj.at[j, pl.ds(o.col, 4)], o.major_l)]
            across = [o.col]
        elif stage == 3:
            sent = [
                (obj.at[j, pl.ds(o.col_l, 2)], o.major_r),
                (obj.at[j, pl.ds(o.col_r + 2, 2)], o.major_l),
            ]
            across = [o.col_r, o.col_l]
        else:
            sent = []
            across = [o.col_o]
        for src, dev in sent:
            frame_copy(src, src, g_send.at[j], g_recv.at[j, stage], dev).start()
        for col in across:
            src = obj.at[j, pl.ds(col, 4)]
            frame_copy(src, src, g_send.at[j], g_recv.at[j, 4], dev_sib).start()

    def gather_wait(j, stage):
        blocks = obj.at[j, pl.ds(0, (2, 1, 8, 4, 16)[stage])]
        frame_copy(blocks, blocks, g_send.at[j], g_recv.at[j, stage], dev_sib).wait_recv()

    def gather_next(j, stage):
        gather_wait(j, stage)
        gather_start(j, stage + 1)

    groups = ((0, 2), (2, 1), (3, 1))

    def reduce_start(g, stage):
        first, count = groups[g]
        o = order(first)
        here = pl.ds(first, count)
        if stage == 0:
            sent = [
                (term.at[here, pl.ds(sib_at + col, 4)], land_a.at[here, pl.ds(col, 4)], dev_sib)
                for col in [at - core_at for at in (o.col_o, o.col_r, o.col_l, o.col)]
            ]
        elif stage == 1:
            sent = [
                (term.at[here, pl.ds(o.col_o, 2)], land_b1.at[0, here], o.major_r),
                (term.at[here, pl.ds(o.col_o + 2, 2)], land_b1.at[1, here], o.major_l),
            ]
        elif stage == 2:
            sent = [
                (term.at[here, pl.ds(o.col_r, 4)], land_b2.at[0, here], o.major_r),
                (term.at[here, pl.ds(o.col_l, 4)], land_b2.at[1, here], o.major_l),
            ]
        elif stage == 3:
            sent = [
                (term.at[here, o.own_o, 0], land_c1.at[0, here], o.minor_r),
                (term.at[here, o.own_o, 1], land_c1.at[1, here], o.minor_l),
            ]
        else:
            sent = [
                (term.at[here, o.own_r], land_c2.at[0, here], o.minor_r),
                (term.at[here, o.own_l], land_c2.at[1, here], o.minor_l),
            ]
        for src, land, dev in sent:
            frame_copy(src, land, r_send.at[g], r_recv.at[g, stage], dev).start()

    def reduce_finish(g, stage):
        first, count = groups[g]
        o = order(first)
        here = pl.ds(first, count)
        blocks = term.at[here, pl.ds(0, (16, 4, 8, 1, 2)[stage])]
        frame_copy(blocks, blocks, r_send.at[g], r_recv.at[g, stage], dev_sib).wait_recv()
        for j in range(first, first + count):
            if stage == 0:
                at = pl.ds(core_at, 16)
                term[j, at] = term[j, at] + land_a[j]
            elif stage == 1:
                there, other = pl.ds(o.col_r, 2), pl.ds(o.col_l + 2, 2)
                term[j, there] = term[j, there] + land_b1[0, j]
                term[j, other] = term[j, other] + land_b1[1, j]
            elif stage == 2:
                at = pl.ds(o.col, 4)
                term[j, at] = term[j, at] + (land_b2[0, j] + land_b2[1, j])
            elif stage == 3:
                term[j, o.own_r, 0] = term[j, o.own_r, 0] + land_c1[0, j]
                term[j, o.own_l, 1] = term[j, o.own_l, 1] + land_c1[1, j]
            else:
                grad_ref[j] = term[j, o.own] + (land_c2[0, j] + land_c2[1, j])

    def reduce_next(g, stage):
        reduce_finish(g, stage)
        reduce_start(g, stage + 1)

    def each_peer(body):
        def run(step, carry):
            body(step)
            return carry

        lax.fori_loop(1, n_chan, run, 0)

    def peers_wait(phase, blocks, sent):
        copy = chan_copy(blocks, blocks, phase, peer(1))
        if sent:
            copy.wait_send()
        else:
            copy.wait_recv()

    others = pl.ds(0, n_chan - 1)
    each_peer(lambda step: chan_copy(phases.at[me], phases.at[me], 0, peer(step)).start())
    sequence = (3, 0, 1, 2)
    for j in sequence:
        gather_start(j, 0)

    amp_copy.wait()
    scale_copy.wait()
    line = lax.broadcasted_iota(jnp.int32, (PUPIL, PUPIL), 0).astype(F32) - (PUPIL - 1) / 2.0
    column = lax.broadcasted_iota(jnp.int32, (PUPIL, PUPIL), 1).astype(F32) - (PUPIL - 1) / 2.0
    inside = line * line + column * column <= (PUPIL / 2.0) ** 2
    aperture = jnp.where(inside, amp[...], 0.0)
    total = jnp.sum(aperture * aperture, axis=(0, 1), keepdims=True)
    inverse = 1.0 / (total * float(GRID * GRID))

    for stage in (0, 1):
        for j in sequence:
            gather_next(j, stage)
    peers_wait(0, phases.at[others], False)
    tab_copy.wait()

    def table(k):
        return tab[0, k].astype(BF16), tab[1, k].astype(BF16)

    def each_channel(body):
        def run(j, carry):
            body(j)
            return carry

        lax.fori_loop(0, channels, run, 0)

    def each_half(body):
        def run(i, carry):
            body(lax.div(i, 2), lax.rem(i, 2))
            return carry

        lax.fori_loop(0, 2 * channels, run, 0)

    wave = phases[...].reshape(PUPIL, PUPIL)

    def fields(j):
        sin_v, cos_v = sincos(scale[j] * wave)
        real, imag = aperture * cos_v, aperture * sin_v
        pupil[j, :, 0:PUPIL] = real
        pupil[j, :, PUPIL:GRID] = imag

    each_channel(fields)

    def pupil_rows(j):
        x_hi, x_lo = split(pupil[j])
        real = dot3(x_hi, x_lo, *table(T_A))
        imag = dot3(x_hi, x_lo, *table(T_B))
        half[j, 0, 0:PUPIL, :] = real
        half[j, 0, PUPIL:GRID, :] = imag
        half[j, 1, 0:PUPIL, :] = imag
        half[j, 1, PUPIL:GRID, :] = -real

    each_channel(pupil_rows)
    gather_next(0, 2)
    gather_next(3, 2)

    def to_spread(j, n):
        spread[j, n] = dot3(*table(T_L2), *split(half[j, n]))

    each_half(to_spread)
    gather_next(1, 2)
    gather_next(0, 3)

    def fold(j):
        real, imag = spread[j, 0], spread[j, 1]
        folded[j] = dot3(*split((real * real + imag * imag) * inverse), *table(T_H))

    each_channel(fold)
    gather_next(2, 2)
    gather_next(1, 3)

    def products(j, t):
        product[j, t] = dot3(*table(T_C + t), *split(folded[j]))

    each_half(products)
    gather_next(3, 3)
    gather_next(2, 3)
    img_copy.wait()

    lane0 = lax.broadcasted_iota(jnp.int32, (16, PUPIL), 1) == 0

    def residual_block(p, s, b):
        j = 2 * p + s
        at = pl.ds(pl.multiple_of(b * 16, 16), 16)
        crossed = lax.rem(b, 4) * 4 + lax.div(b, 4)
        k = jnp.where(j == last, crossed, b) if s == 1 else b
        o_r = jnp.concatenate([obj[j, k, 0], obj[j, k + 16, 0]], 0)
        o_i = jnp.concatenate([obj[j, k, 1], obj[j, k + 16, 1]], 0)
        p1, p3 = product[j, 0, at, 0:PUPIL], product[j, 0, at, PUPIL:GRID]
        p4, p2 = product[j, 1, at, 0:PUPIL], product[j, 1, at, PUPIL:GRID]
        t_r = jnp.concatenate(
            [p1 + jnp.where(lane0, 0.0, p2), mirror(jnp.where(lane0, p3, p1 - p2))], 1
        )
        t_i = jnp.concatenate(
            [jnp.where(lane0, 0.0, p3) - p4, mirror(jnp.where(lane0, -p2, -p3 - p4))], 1
        )
        r_r = o_r * t_r - o_i * t_i - img[j, 0, 0, at, :]
        r_i = o_r * t_i + o_i * t_r - img[j, 0, 1, at, :]
        g_r = t_r * r_r + t_i * r_i
        g_i = t_r * r_i - t_i * r_r
        term[j, k, 0] = g_r[0:8]
        term[j, k + 16, 0] = g_r[8:16]
        term[j, k, 1] = g_i[0:8]
        term[j, k + 16, 1] = g_i[8:16]
        w_r = o_r * r_r + o_i * r_i
        w_i = o_r * r_i - o_i * r_r
        wr_p, wi_p = w_r[:, 0:PUPIL], w_i[:, 0:PUPIL]
        wr_m, wi_m = mirror(w_r[:, PUPIL:GRID]), mirror(w_i[:, PUPIL:GRID])
        top = jnp.concatenate(
            [wr_p + jnp.where(lane0, 0.0, wr_m), jnp.where(lane0, wr_m, wi_p - wi_m)], 1
        )
        low = jnp.concatenate(
            [-(wi_p + jnp.where(lane0, 0.0, wi_m)), jnp.where(lane0, -wi_m, wr_p - wr_m)], 1
        )
        weight[j, 0, at, :] = top
        weight[j, 1, at, :] = low

    def residual(p):
        def run(b, carry):
            for s in range(2):
                residual_block(p, s, b)
            return carry

        lax.fori_loop(0, GRID // 16, run, 0, unroll=2)

    def pair_residual(p, carry):
        gather_wait(2 * p, 4)
        gather_wait(2 * p + 1, 4)
        residual(p)

        @pl.when(p == 0)
        def _():
            reduce_start(0, 0)

        @pl.when(p == 1)
        def _():
            reduce_start(1, 0)
            reduce_start(2, 0)

        return carry

    lax.fori_loop(0, pairs, pair_residual, 0)

    def unproducts(j, t):
        back[j, t] = dot3(*table(T_C + t), *split(weight[j, t]))

    each_half(unproducts)
    reduce_next(0, 0)

    def unfold(j):
        change = dot3(*split(back[j, 0] + back[j, 1]), *table(T_HT)) * (2.0 * inverse)
        along[j, 0] = change * spread[j, 0]
        along[j, 1] = change * spread[j, 1]

    each_channel(unfold)
    reduce_next(1, 0)
    reduce_next(2, 0)
    reduce_next(0, 1)

    def from_spread(j, n):
        last_rows[j, n] = dot3(*split(along[j, n]), *table(T_BACK + n))

    each_half(from_spread)
    reduce_next(1, 1)
    reduce_next(2, 1)
    reduce_next(0, 2)
    pgrad[...] = jnp.zeros_like(pgrad)

    def to_pupil(j):
        g = dot3(*table(T_A), *split(last_rows[j, 0] + last_rows[j, 1]))
        g_r = g[0:PUPIL, 0:PUPIL] - g[PUPIL:GRID, PUPIL:GRID]
        g_i = g[PUPIL:GRID, 0:PUPIL] + g[0:PUPIL, PUPIL:GRID]
        change = scale[j] * (pupil[j, :, 0:PUPIL] * g_i - pupil[j, :, PUPIL:GRID] * g_r)
        pgrad[...] = pgrad[...] + change.reshape(pgrad.shape)

    each_channel(to_pupil)
    each_peer(lambda step: chan_copy(pgrad.at[peer(step)], land_pg.at[step], 1, peer(step)).start())
    reduce_next(0, 3)
    reduce_next(1, 2)
    reduce_next(2, 2)

    part[...] = jnp.zeros_like(part)
    peers_wait(1, land_pg.at[others], False)
    summed = pgrad[me]
    for step in range(1, n_chan):
        summed = summed + land_pg[step]
    for m in range(modes):
        part[m : m + 1, :] = jnp.sum(maps[m] * summed, axis=0, keepdims=True)
    vec[...] = lax.dot_general(
        jnp.ones((8, PUPIL), F32),
        part[...],
        (((1,), (1,)), ((), ())),
        precision=lax.Precision.HIGHEST,
        preferred_element_type=F32,
    )
    each_peer(lambda step: chan_copy(vec, land_vec.at[step], 2, peer(step)).start())
    reduce_next(1, 3)
    reduce_next(2, 3)
    reduce_finish(0, 4)
    peers_wait(2, land_vec.at[others], False)
    answer = vec[...]
    for step in range(1, n_chan):
        answer = answer + land_vec[step]
    mode_ref[...] = answer[0:1, 0:modes]
    reduce_finish(1, 4)
    reduce_finish(2, 4)

    for j in range(channels):
        blocks = obj.at[j, pl.ds(0, 31)]
        frame_copy(blocks, blocks, g_send.at[j], g_recv.at[j, 0], dev_sib).wait_send()
    for g, (first, count) in enumerate(groups):
        blocks = term.at[pl.ds(first, count), pl.ds(0, 31)]
        frame_copy(blocks, blocks, r_send.at[g], r_recv.at[g, 0], dev_sib).wait_send()
    peers_wait(0, phases.at[others], True)
    peers_wait(1, land_pg.at[others], True)
    peers_wait(2, land_vec.at[others], True)


def on_device(n_chan, images, objects, coeffs, mode_maps, amplitude, phase_scale):
    channels = images.shape[0]
    modes = coeffs.shape[1]
    rows = mode_maps.shape[1]
    vmem = pl.BlockSpec(memory_space=pltpu.VMEM)
    hbm = pl.BlockSpec(memory_space=pltpu.HBM)
    dma = pltpu.SemaphoreType.DMA
    block = (2, 8, GRID)
    outs = (
        jax.ShapeDtypeStruct(objects.shape, F32),
        jax.ShapeDtypeStruct(coeffs.shape, F32),
    )
    inputs = (images, objects, coeffs, mode_maps, amplitude, phase_scale, jnp.asarray(build_tables()))
    return pl.pallas_call(
        functools.partial(kernel, n_chan, channels, modes),
        out_shape=outs,
        in_specs=[hbm] * 7,
        out_specs=(vmem, vmem),
        scratch_shapes=[
            pltpu.SMEM(coeffs.shape, F32),
            pltpu.SMEM(phase_scale.shape, F32),
            pltpu.VMEM(mode_maps.shape, F32),
            pltpu.VMEM(amplitude.shape, F32),
            pltpu.VMEM(images.shape, F32),
            pltpu.VMEM((2, 9, GRID, GRID), F32),
            pltpu.VMEM((channels, 32) + block, F32),
            pltpu.VMEM((channels, 32) + block, F32),
            pltpu.VMEM((channels, 16) + block, F32),
            pltpu.VMEM((2, channels, 2) + block, F32),
            pltpu.VMEM((2, channels, 4) + block, F32),
            pltpu.VMEM((2, channels, 8, GRID), F32),
            pltpu.VMEM((2, channels) + block, F32),
            pltpu.VMEM((n_chan, rows, PUPIL), F32),
            pltpu.VMEM((channels, PUPIL, GRID), F32),
            pltpu.VMEM((channels, 2, GRID, GRID), F32),
            pltpu.VMEM((channels, 2, GRID, GRID), F32),
            pltpu.VMEM((channels, GRID, GRID), F32),
            pltpu.VMEM((channels, 2, GRID, GRID), F32),
            pltpu.VMEM((channels, 2, GRID, GRID), F32),
            pltpu.VMEM((channels, 2, GRID, GRID), F32),
            pltpu.VMEM((channels, 2, GRID, GRID), F32),
            pltpu.VMEM((channels, 2, GRID, GRID), F32),
            pltpu.VMEM((n_chan, rows, PUPIL), F32),
            pltpu.VMEM((n_chan, rows, PUPIL), F32),
            pltpu.VMEM((PUPIL, PUPIL), F32),
            pltpu.VMEM((8, PUPIL), F32),
            pltpu.VMEM((n_chan, 8, PUPIL), F32),
            dma((8,)),
            dma((3,)),
            dma((3,)),
            dma((channels,)),
            dma((channels, 5)),
            dma((3,)),
            dma((3, 5)),
        ],
        compiler_params=pltpu.CompilerParams(
            collective_id=0, has_side_effects=True, vmem_limit_bytes=48 * 1024 * 1024
        ),
        name="deconvolve",
    )(*[pltpu.with_memory_space_constraint(value, pltpu.HBM) for value in inputs])


def solution(mesh):
    return jax.shard_map(
        functools.partial(on_device, mesh.shape["chan"]),
        mesh=mesh,
        in_specs=(
            P("chan", "frame", None, None, None),
            P("chan", None, "frame", None),
            P("frame", None),
            P(None, "chan", None),
            P(),
            P("chan"),
        ),
        out_specs=(P("chan", None, "frame", None), P("frame", None)),
        check_vma=False,
    )
```

```python
import functools
import math

import jax
import jax.numpy as jnp
import numpy as np
from jax import lax
from jax.experimental import pallas as pl
from jax.experimental.pallas import tpu as pltpu
from jax.sharding import PartitionSpec as P

F32 = jnp.float32
BF16 = jnp.bfloat16
MESH = pl.DeviceIdType.MESH
GRID = 256
PUPIL = 128

T_A, T_B, T_L2, T_H, T_C, T_S, T_HT, T_BACK = 0, 1, 2, 3, 4, 5, 6, 7


def build_tables():
    index = np.arange(GRID)
    turn = (np.outer(index, index) % GRID) * (2.0 * math.pi / GRID)
    cos, sin = np.cos(turn), np.sin(turn)
    half = PUPIL
    first = np.concatenate([cos[:half], sin[:half]], 0)
    second = np.concatenate([-sin[:half], cos[:half]], 0)
    left = np.concatenate([cos[:, :half], sin[:, :half]], 1)
    minus = -sin[:, :half]
    minus[:, 0] = cos[:, half]
    herm = np.concatenate([cos[:, :half], minus], 1)
    back = np.concatenate(
        [
            np.concatenate([cos[:, :half], sin[:, :half]], 1),
            np.concatenate([-sin[:, :half], cos[:, :half]], 1),
        ],
        0,
    )
    table = np.concatenate([first, second, left, herm, cos, sin, herm.T, back], 0)
    return table.astype(np.float32).reshape(-1, GRID, GRID)


def split(value):
    high = value.astype(BF16)
    low = (value - high.astype(F32)).astype(BF16)
    return high, low


def dot(a, b):
    return jnp.dot(a, b, preferred_element_type=F32)


def dot3(a_high, a_low, b_high, b_low):
    left = jnp.concatenate([a_high, a_low, a_high], 1)
    right = jnp.concatenate([b_high, b_high, b_low], 0)
    return dot(left, right)


def sincos(angle):
    k = jnp.floor(angle * (2.0 / math.pi) + 0.5)
    r = ((angle - k * 1.5703125) - k * 4.837512969970703125e-4) - k * 7.54978995489188216e-8
    z = r * r
    sin_r = ((-1.9515295891e-4 * z + 8.3321608736e-3) * z - 1.6666654611e-1) * z * r + r
    cos_r = ((2.443315711809948e-5 * z - 1.388731625493765e-3) * z + 4.166664568298827e-2) * z * z - 0.5 * z + 1.0
    quad = k - 4.0 * jnp.floor(k * 0.25)
    odd = (quad == 1.0) | (quad == 3.0)
    sin_v = jnp.where(odd, cos_r, sin_r)
    cos_v = jnp.where(odd, sin_r, cos_r)
    sin_v = jnp.where(quad >= 2.0, -sin_v, sin_v)
    cos_v = jnp.where((quad == 1.0) | (quad == 2.0), -cos_v, cos_v)
    return sin_v, cos_v


def mirror(value):
    lane = lax.broadcasted_iota(jnp.int32, value.shape, 1)
    index = (PUPIL - lane) & (PUPIL - 1)
    return jnp.take_along_axis(value, index, axis=1, mode="promise_in_bounds")


def kernel(
    n_chan,
    channels,
    modes,
    images_hbm,
    objects_hbm,
    coeffs_hbm,
    maps_hbm,
    amp_hbm,
    scale_hbm,
    table_hbm,
    grad_ref,
    mode_ref,
    coeffs,
    scale,
    maps,
    amp,
    img,
    tab,
    obj,
    term,
    land_a,
    land_b1,
    land_b2,
    land_c1,
    land_c2,
    phases,
    pupil,
    half,
    spread,
    folded,
    product,
    weight,
    back,
    along,
    last_rows,
    pgrad,
    land_pg,
    part,
    vec,
    land_vec,
    local_sem,
    peer_send,
    peer_recv,
    g_send,
    g_recv,
    r_send,
    r_recv,
):
    pairs = channels // 2
    me = lax.axis_index("chan")
    fr = lax.axis_index("frame")
    cx = lax.div(fr, 8)
    cy = lax.rem(lax.div(fr, 2), 4)
    cc = lax.rem(fr, 2)
    x_r, x_l = lax.rem(cx + 1, 4), lax.rem(cx + 3, 4)
    y_r, y_l = lax.rem(cy + 1, 4), lax.rem(cy + 3, 4)
    sib = 1 - cc
    dev_xr = x_r * 8 + cy * 2 + cc
    dev_xl = x_l * 8 + cy * 2 + cc
    dev_yr = cx * 8 + y_r * 2 + cc
    dev_yl = cx * 8 + y_l * 2 + cc
    dev_sib = cx * 8 + cy * 2 + sib
    core_at = cc * 16
    sib_at = sib * 16

    class Order:
        def __init__(self, major, minor, devices):
            self.col, self.col_r, self.col_l, self.col_o = [
                core_at + lax.rem(major + step, 4) * 4 for step in (0, 1, 3, 2)
            ]
            self.own, self.own_r, self.own_l, self.own_o = [
                self.col + lax.rem(minor + step, 4) for step in (0, 1, 3, 2)
            ]
            self.major_r, self.major_l, self.minor_r, self.minor_l = devices

    by_column = Order(cx, cy, (dev_xr, dev_xl, dev_yr, dev_yl))
    by_row = Order(cy, cx, (dev_yr, dev_yl, dev_xr, dev_xl))
    last = channels - 1

    def order(j):
        return by_row if j == last else by_column

    def peer(step):
        return lax.rem(me + step, n_chan)

    def local(k, src, dst):
        copy = pltpu.make_async_copy(src, dst, local_sem.at[k])
        copy.start(priority=1)
        return copy

    maps_copy = local(0, maps_hbm, maps)
    coeffs_copy = local(1, coeffs_hbm, coeffs)
    obj_copies = [
        local(2, objects_hbm.at[pl.ds(0, last)], obj.at[pl.ds(0, last), by_column.own]),
        local(7, objects_hbm.at[last], obj.at[last, by_row.own]),
    ]
    scale_copy = local(3, scale_hbm, scale)
    amp_copy = local(4, amp_hbm, amp)
    tab_copy = local(5, table_hbm, tab)
    img_copy = local(6, images_hbm, img)
    barrier = pltpu.get_barrier_semaphore()
    for dev in (dev_yr, dev_yl, dev_xr, dev_xl, dev_sib):
        pl.semaphore_signal(barrier, inc=1, device_id={"frame": dev}, device_id_type=MESH)
    for step in range(1, n_chan):
        pl.semaphore_signal(barrier, inc=1, device_id={"chan": peer(step)}, device_id_type=MESH)

    maps_copy.wait()
    coeffs_copy.wait()
    mine = coeffs[0, 0] * maps[0]
    for m in range(1, modes):
        mine = mine + coeffs[0, m] * maps[m]
    phases[me] = mine
    for copy in obj_copies:
        copy.wait()
    pl.semaphore_wait(barrier, 5 + n_chan - 1)

    def frame_copy(src, dst, send, recv, dev):
        return pltpu.make_async_remote_copy(
            src_ref=src,
            dst_ref=dst,
            send_sem=send,
            recv_sem=recv,
            device_id={"frame": dev},
            device_id_type=MESH,
        )

    def chan_copy(src, dst, phase, dev):
        return pltpu.make_async_remote_copy(
            src_ref=src,
            dst_ref=dst,
            send_sem=peer_send.at[phase],
            recv_sem=peer_recv.at[phase],
            device_id={"chan": dev},
            device_id_type=MESH,
        )

    def gather_start(j, stage):
        o = order(j)
        across = []
        if stage == 0:
            sent = [(obj.at[j, o.own], o.minor_r), (obj.at[j, o.own], o.minor_l)]
        elif stage == 1:
            sent = [(obj.at[j, o.own_l, 0], o.minor_r), (obj.at[j, o.own_r, 1], o.minor_l)]
        elif stage == 2:
            sent = [(obj.at[j, pl.ds(o.col, 4)], o.major_r), (obj.at[j, pl.ds(o.col, 4)], o.major_l)]
            across = [o.col]
        elif stage == 3:
            sent = [
                (obj.at[j, pl.ds(o.col_l, 2)], o.major_r),
                (obj.at[j, pl.ds(o.col_r + 2, 2)], o.major_l),
            ]
            across = [o.col_r, o.col_l]
        else:
            sent = []
            across = [o.col_o]
        for src, dev in sent:
            frame_copy(src, src, g_send.at[j], g_recv.at[j, stage], dev).start()
        for col in across:
            src = obj.at[j, pl.ds(col, 4)]
            frame_copy(src, src, g_send.at[j], g_recv.at[j, 4], dev_sib).start()

    def gather_wait(j, stage):
        blocks = obj.at[j, pl.ds(0, (2, 1, 8, 4, 16)[stage])]
        frame_copy(blocks, blocks, g_send.at[j], g_recv.at[j, stage], dev_sib).wait_recv()

    def gather_next(j, stage):
        gather_wait(j, stage)
        gather_start(j, stage + 1)

    groups = ((0, 2), (2, 1), (3, 1))

    def reduce_start(g, stage):
        first, count = groups[g]
        o = order(first)
        here = pl.ds(first, count)
        if stage == 0:
            sent = [
                (term.at[here, pl.ds(sib_at + col, 4)], land_a.at[here, pl.ds(col, 4)], dev_sib)
                for col in [at - core_at for at in (o.col_o, o.col_r, o.col_l, o.col)]
            ]
        elif stage == 1:
            sent = [
                (term.at[here, pl.ds(o.col_o, 2)], land_b1.at[0, here], o.major_r),
                (term.at[here, pl.ds(o.col_o + 2, 2)], land_b1.at[1, here], o.major_l),
            ]
        elif stage == 2:
            sent = [
                (term.at[here, pl.ds(o.col_r, 4)], land_b2.at[0, here], o.major_r),
                (term.at[here, pl.ds(o.col_l, 4)], land_b2.at[1, here], o.major_l),
            ]
        elif stage == 3:
            sent = [
                (term.at[here, o.own_o, 0], land_c1.at[0, here], o.minor_r),
                (term.at[here, o.own_o, 1], land_c1.at[1, here], o.minor_l),
            ]
        else:
            sent = [
                (term.at[here, o.own_r], land_c2.at[0, here], o.minor_r),
                (term.at[here, o.own_l], land_c2.at[1, here], o.minor_l),
            ]
        for src, land, dev in sent:
            frame_copy(src, land, r_send.at[g], r_recv.at[g, stage], dev).start()

    def reduce_finish(g, stage):
        first, count = groups[g]
        o = order(first)
        here = pl.ds(first, count)
        blocks = term.at[here, pl.ds(0, (16, 4, 8, 1, 2)[stage])]
        frame_copy(blocks, blocks, r_send.at[g], r_recv.at[g, stage], dev_sib).wait_recv()
        for j in range(first, first + count):
            if stage == 0:
                at = pl.ds(core_at, 16)
                term[j, at] = term[j, at] + land_a[j]
            elif stage == 1:
                there, other = pl.ds(o.col_r, 2), pl.ds(o.col_l + 2, 2)
                term[j, there] = term[j, there] + land_b1[0, j]
                term[j, other] = term[j, other] + land_b1[1, j]
            elif stage == 2:
                at = pl.ds(o.col, 4)
                term[j, at] = term[j, at] + (land_b2[0, j] + land_b2[1, j])
            elif stage == 3:
                term[j, o.own_r, 0] = term[j, o.own_r, 0] + land_c1[0, j]
                term[j, o.own_l, 1] = term[j, o.own_l, 1] + land_c1[1, j]
            else:
                grad_ref[j] = term[j, o.own] + (land_c2[0, j] + land_c2[1, j])

    def reduce_next(g, stage):
        reduce_finish(g, stage)
        reduce_start(g, stage + 1)

    def each_peer(body):
        def run(step, carry):
            body(step)
            return carry

        lax.fori_loop(1, n_chan, run, 0)

    def peers_wait(phase, blocks, sent):
        copy = chan_copy(blocks, blocks, phase, peer(1))
        if sent:
            copy.wait_send()
        else:
            copy.wait_recv()

    others = pl.ds(0, n_chan - 1)
    each_peer(lambda step: chan_copy(phases.at[me], phases.at[me], 0, peer(step)).start())
    sequence = (3, 0, 1, 2)
    for j in sequence:
        gather_start(j, 0)

    amp_copy.wait()
    scale_copy.wait()
    line = lax.broadcasted_iota(jnp.int32, (PUPIL, PUPIL), 0).astype(F32) - (PUPIL - 1) / 2.0
    column = lax.broadcasted_iota(jnp.int32, (PUPIL, PUPIL), 1).astype(F32) - (PUPIL - 1) / 2.0
    inside = line * line + column * column <= (PUPIL / 2.0) ** 2
    aperture = jnp.where(inside, amp[...], 0.0)
    total = jnp.sum(aperture * aperture, axis=(0, 1), keepdims=True)
    inverse = 1.0 / (total * float(GRID * GRID))

    for stage in (0, 1):
        for j in sequence:
            gather_next(j, stage)
    peers_wait(0, phases.at[others], False)
    tab_copy.wait()

    def table(k):
        return split(tab[k])

    def each_channel(body):
        def run(j, carry):
            body(j)
            return carry

        lax.fori_loop(0, channels, run, 0)

    def at_turn(j, turn, steps):
        @pl.when(j == turn)
        def _():
            for step, which, stage in steps:
                step(which, stage)

    wave = phases[...].reshape(PUPIL, PUPIL)

    def fields(j):
        sin_v, cos_v = sincos(scale[j] * wave)
        real, imag = aperture * cos_v, aperture * sin_v
        pupil[j, :, 0:PUPIL] = real
        pupil[j, :, PUPIL:GRID] = imag

    each_channel(fields)

    def pupil_rows(j):
        x_hi, x_lo = split(pupil[j])
        real = dot3(x_hi, x_lo, *table(T_A))
        imag = dot3(x_hi, x_lo, *table(T_B))
        half[j, 0, 0:PUPIL, :] = real
        half[j, 0, PUPIL:GRID, :] = imag
        half[j, 1, 0:PUPIL, :] = imag
        half[j, 1, PUPIL:GRID, :] = -real

    each_channel(pupil_rows)

    def to_spread(j):
        l_hi, l_lo = table(T_L2)
        for n in range(2):
            spread[j, n] = dot3(l_hi, l_lo, *split(half[j, n]))
        at_turn(j, 0, [(gather_next, 0, 2)])
        at_turn(j, 1, [(gather_next, 1, 2), (gather_next, 3, 2)])
        at_turn(j, 2, [(gather_next, 2, 2), (gather_next, 0, 3)])
        at_turn(j, 3, [(gather_next, 1, 3)])

    each_channel(to_spread)

    def fold(j):
        real, imag = spread[j, 0], spread[j, 1]
        folded[j] = dot3(*split((real * real + imag * imag) * inverse), *table(T_H))
        at_turn(j, 1, [(gather_next, 3, 3)])
        at_turn(j, 3, [(gather_next, 2, 3)])

    each_channel(fold)

    def products(j):
        q_hi, q_lo = split(folded[j])
        for t in range(2):
            product[j, t] = dot3(*table(T_C + t), q_hi, q_lo)

    each_channel(products)
    img_copy.wait()

    lane0 = lax.broadcasted_iota(jnp.int32, (16, PUPIL), 1) == 0

    def residual_block(p, s, b):
        j = 2 * p + s
        at = pl.ds(pl.multiple_of(b * 16, 16), 16)
        crossed = lax.rem(b, 4) * 4 + lax.div(b, 4)
        k = jnp.where(j == last, crossed, b) if s == 1 else b
        o_r = jnp.concatenate([obj[j, k, 0], obj[j, k + 16, 0]], 0)
        o_i = jnp.concatenate([obj[j, k, 1], obj[j, k + 16, 1]], 0)
        p1, p3 = product[j, 0, at, 0:PUPIL], product[j, 0, at, PUPIL:GRID]
        p4, p2 = product[j, 1, at, 0:PUPIL], product[j, 1, at, PUPIL:GRID]
        t_r = jnp.concatenate(
            [p1 + jnp.where(lane0, 0.0, p2), mirror(jnp.where(lane0, p3, p1 - p2))], 1
        )
        t_i = jnp.concatenate(
            [jnp.where(lane0, 0.0, p3) - p4, mirror(jnp.where(lane0, -p2, -p3 - p4))], 1
        )
        r_r = o_r * t_r - o_i * t_i - img[j, 0, 0, at, :]
        r_i = o_r * t_i + o_i * t_r - img[j, 0, 1, at, :]
        g_r = t_r * r_r + t_i * r_i
        g_i = t_r * r_i - t_i * r_r
        term[j, k, 0] = g_r[0:8]
        term[j, k + 16, 0] = g_r[8:16]
        term[j, k, 1] = g_i[0:8]
        term[j, k + 16, 1] = g_i[8:16]
        w_r = o_r * r_r + o_i * r_i
        w_i = o_r * r_i - o_i * r_r
        wr_p, wi_p = w_r[:, 0:PUPIL], w_i[:, 0:PUPIL]
        wr_m, wi_m = mirror(w_r[:, PUPIL:GRID]), mirror(w_i[:, PUPIL:GRID])
        top = jnp.concatenate(
            [wr_p + jnp.where(lane0, 0.0, wr_m), jnp.where(lane0, wr_m, wi_p - wi_m)], 1
        )
        low = jnp.concatenate(
            [-(wi_p + jnp.where(lane0, 0.0, wi_m)), jnp.where(lane0, -wi_m, wr_p - wr_m)], 1
        )
        weight[j, 0, at, :] = top
        weight[j, 1, at, :] = low

    def residual(p):
        def run(b, carry):
            for s in range(2):
                residual_block(p, s, b)
            return carry

        lax.fori_loop(0, GRID // 16, run, 0, unroll=2)

    def pair_residual(p, carry):
        gather_wait(2 * p, 4)
        gather_wait(2 * p + 1, 4)
        residual(p)

        @pl.when(p == 0)
        def _():
            reduce_start(0, 0)

        @pl.when(p == 1)
        def _():
            reduce_start(1, 0)
            reduce_start(2, 0)

        return carry

    lax.fori_loop(0, pairs, pair_residual, 0)

    def unproducts(j):
        for t in range(2):
            back[j, t] = dot3(*table(T_C + t), *split(weight[j, t]))
        at_turn(j, 0, [(reduce_next, 0, 0)])
        at_turn(j, 2, [(reduce_next, 1, 0), (reduce_next, 2, 0)])

    each_channel(unproducts)

    def unfold(j):
        change = dot3(*split(back[j, 0] + back[j, 1]), *table(T_HT)) * (2.0 * inverse)
        along[j, 0] = change * spread[j, 0]
        along[j, 1] = change * spread[j, 1]
        at_turn(j, 1, [(reduce_next, 0, 1)])
        at_turn(j, 3, [(reduce_next, 1, 1), (reduce_next, 2, 1)])

    each_channel(unfold)

    def from_spread(j):
        for n in range(2):
            last_rows[j, n] = dot3(*split(along[j, n]), *table(T_BACK + n))
        at_turn(j, 1, [(reduce_next, 0, 2)])
        at_turn(j, 3, [(reduce_next, 1, 2), (reduce_next, 2, 2)])

    each_channel(from_spread)
    pgrad[...] = jnp.zeros_like(pgrad)

    def to_pupil(j):
        g = dot3(*table(T_A), *split(last_rows[j, 0] + last_rows[j, 1]))
        g_r = g[0:PUPIL, 0:PUPIL] - g[PUPIL:GRID, PUPIL:GRID]
        g_i = g[PUPIL:GRID, 0:PUPIL] + g[0:PUPIL, PUPIL:GRID]
        change = scale[j] * (pupil[j, :, 0:PUPIL] * g_i - pupil[j, :, PUPIL:GRID] * g_r)
        pgrad[...] = pgrad[...] + change.reshape(pgrad.shape)
        at_turn(j, 2, [(reduce_next, 0, 3)])

    each_channel(to_pupil)
    each_peer(lambda step: chan_copy(pgrad.at[peer(step)], land_pg.at[step], 1, peer(step)).start())
    reduce_next(1, 3)
    reduce_next(2, 3)

    part[...] = jnp.zeros_like(part)
    peers_wait(1, land_pg.at[others], False)
    summed = pgrad[me]
    for step in range(1, n_chan):
        summed = summed + land_pg[step]
    for m in range(modes):
        part[m : m + 1, :] = jnp.sum(maps[m] * summed, axis=0, keepdims=True)
    vec[...] = lax.dot_general(
        jnp.ones((8, PUPIL), F32),
        part[...],
        (((1,), (1,)), ((), ())),
        precision=lax.Precision.HIGHEST,
        preferred_element_type=F32,
    )
    each_peer(lambda step: chan_copy(vec, land_vec.at[step], 2, peer(step)).start())
    reduce_finish(0, 4)
    peers_wait(2, land_vec.at[others], False)
    answer = vec[...]
    for step in range(1, n_chan):
        answer = answer + land_vec[step]
    mode_ref[...] = answer[0:1, 0:modes]
    reduce_finish(1, 4)
    reduce_finish(2, 4)

    for j in range(channels):
        blocks = obj.at[j, pl.ds(0, 31)]
        frame_copy(blocks, blocks, g_send.at[j], g_recv.at[j, 0], dev_sib).wait_send()
    for g, (first, count) in enumerate(groups):
        blocks = term.at[pl.ds(first, count), pl.ds(0, 31)]
        frame_copy(blocks, blocks, r_send.at[g], r_recv.at[g, 0], dev_sib).wait_send()
    peers_wait(0, phases.at[others], True)
    peers_wait(1, land_pg.at[others], True)
    peers_wait(2, land_vec.at[others], True)


def on_device(n_chan, images, objects, coeffs, mode_maps, amplitude, phase_scale):
    channels = images.shape[0]
    modes = coeffs.shape[1]
    rows = mode_maps.shape[1]
    vmem = pl.BlockSpec(memory_space=pltpu.VMEM)
    hbm = pl.BlockSpec(memory_space=pltpu.HBM)
    dma = pltpu.SemaphoreType.DMA
    block = (2, 8, GRID)
    outs = (
        jax.ShapeDtypeStruct(objects.shape, F32),
        jax.ShapeDtypeStruct(coeffs.shape, F32),
    )
    inputs = (images, objects, coeffs, mode_maps, amplitude, phase_scale, jnp.asarray(build_tables()))
    return pl.pallas_call(
        functools.partial(kernel, n_chan, channels, modes),
        out_shape=outs,
        in_specs=[hbm] * 7,
        out_specs=(vmem, vmem),
        scratch_shapes=[
            pltpu.SMEM(coeffs.shape, F32),
            pltpu.SMEM(phase_scale.shape, F32),
            pltpu.VMEM(mode_maps.shape, F32),
            pltpu.VMEM(amplitude.shape, F32),
            pltpu.VMEM(images.shape, F32),
            pltpu.VMEM((9, GRID, GRID), F32),
            pltpu.VMEM((channels, 32) + block, F32),
            pltpu.VMEM((channels, 32) + block, F32),
            pltpu.VMEM((channels, 16) + block, F32),
            pltpu.VMEM((2, channels, 2) + block, F32),
            pltpu.VMEM((2, channels, 4) + block, F32),
            pltpu.VMEM((2, channels, 8, GRID), F32),
            pltpu.VMEM((2, channels) + block, F32),
            pltpu.VMEM((n_chan, rows, PUPIL), F32),
            pltpu.VMEM((channels, PUPIL, GRID), F32),
            pltpu.VMEM((channels, 2, GRID, GRID), F32),
            pltpu.VMEM((channels, 2, GRID, GRID), F32),
            pltpu.VMEM((channels, GRID, GRID), F32),
            pltpu.VMEM((channels, 2, GRID, GRID), F32),
            pltpu.VMEM((channels, 2, GRID, GRID), F32),
            pltpu.VMEM((channels, 2, GRID, GRID), F32),
            pltpu.VMEM((channels, 2, GRID, GRID), F32),
            pltpu.VMEM((channels, 2, GRID, GRID), F32),
            pltpu.VMEM((n_chan, rows, PUPIL), F32),
            pltpu.VMEM((n_chan, rows, PUPIL), F32),
            pltpu.VMEM((PUPIL, PUPIL), F32),
            pltpu.VMEM((8, PUPIL), F32),
            pltpu.VMEM((n_chan, 8, PUPIL), F32),
            dma((8,)),
            dma((3,)),
            dma((3,)),
            dma((channels,)),
            dma((channels, 5)),
            dma((3,)),
            dma((3, 5)),
        ],
        compiler_params=pltpu.CompilerParams(
            collective_id=0, has_side_effects=True, vmem_limit_bytes=48 * 1024 * 1024
        ),
        name="deconvolve",
    )(*[pltpu.with_memory_space_constraint(value, pltpu.HBM) for value in inputs])


def solution(mesh):
    return jax.shard_map(
        functools.partial(on_device, mesh.shape["chan"]),
        mesh=mesh,
        in_specs=(
            P("chan", "frame", None, None, None),
            P("chan", None, "frame", None),
            P("frame", None),
            P(None, "chan", None),
            P(),
            P("chan"),
        ),
        out_specs=(P("chan", None, "frame", None), P("frame", None)),
        check_vma=False,
    )
```

```python
import functools
import math

import jax
import jax.numpy as jnp
import ml_dtypes
import numpy as np
from jax import lax
from jax.experimental import pallas as pl
from jax.experimental.pallas import tpu as pltpu
from jax.sharding import PartitionSpec as P

F32 = jnp.float32
BF16 = jnp.bfloat16
MESH = pl.DeviceIdType.MESH
GRID = 256
PUPIL = 128

T_A, T_B, T_L2, T_H, T_C, T_S, T_HT, T_BACK = 0, 1, 2, 3, 4, 5, 6, 7


def build_tables():
    index = np.arange(GRID)
    turn = (np.outer(index, index) % GRID) * (2.0 * math.pi / GRID)
    cos, sin = np.cos(turn), np.sin(turn)
    half = PUPIL
    first = np.concatenate([cos[:half], sin[:half]], 0)
    second = np.concatenate([-sin[:half], cos[:half]], 0)
    left = np.concatenate([cos[:, :half], sin[:, :half]], 1)
    minus = -sin[:, :half]
    minus[:, 0] = cos[:, half]
    herm = np.concatenate([cos[:, :half], minus], 1)
    back = np.concatenate(
        [
            np.concatenate([cos[:, :half], sin[:, :half]], 1),
            np.concatenate([-sin[:, :half], cos[:, :half]], 1),
        ],
        0,
    )
    table = np.concatenate([first, second, left, herm, cos, sin, herm.T, back], 0).astype(np.float32)
    high = table.astype(ml_dtypes.bfloat16)
    high = high.astype(np.float32)
    low = (table - high).astype(ml_dtypes.bfloat16).astype(np.float32)
    return np.stack([high, low]).reshape(2, -1, GRID, GRID)


def split(value):
    high = value.astype(BF16)
    low = (value - high.astype(F32)).astype(BF16)
    return high, low


def dot(a, b):
    return jnp.dot(a, b, preferred_element_type=F32)


def dot3(a_high, a_low, b_high, b_low):
    left = jnp.concatenate([a_high, a_low, a_high], 1)
    right = jnp.concatenate([b_high, b_high, b_low], 0)
    return dot(left, right)


def sincos(angle):
    k = jnp.floor(angle * (2.0 / math.pi) + 0.5)
    r = ((angle - k * 1.5703125) - k * 4.837512969970703125e-4) - k * 7.54978995489188216e-8
    z = r * r
    sin_r = ((-1.9515295891e-4 * z + 8.3321608736e-3) * z - 1.6666654611e-1) * z * r + r
    cos_r = ((2.443315711809948e-5 * z - 1.388731625493765e-3) * z + 4.166664568298827e-2) * z * z - 0.5 * z + 1.0
    quad = k - 4.0 * jnp.floor(k * 0.25)
    odd = (quad == 1.0) | (quad == 3.0)
    sin_v = jnp.where(odd, cos_r, sin_r)
    cos_v = jnp.where(odd, sin_r, cos_r)
    sin_v = jnp.where(quad >= 2.0, -sin_v, sin_v)
    cos_v = jnp.where((quad == 1.0) | (quad == 2.0), -cos_v, cos_v)
    return sin_v, cos_v


def mirror(value):
    lane = lax.broadcasted_iota(jnp.int32, value.shape, 1)
    index = (PUPIL - lane) & (PUPIL - 1)
    return jnp.take_along_axis(value, index, axis=1, mode="promise_in_bounds")


def kernel(
    n_chan,
    channels,
    modes,
    images_hbm,
    objects_hbm,
    coeffs_hbm,
    maps_hbm,
    amp_hbm,
    scale_hbm,
    table_hbm,
    grad_ref,
    mode_ref,
    coeffs,
    scale,
    maps,
    amp,
    img,
    tab,
    obj,
    term,
    land_a,
    land_b1,
    land_b2,
    land_c1,
    land_c2,
    phases,
    pupil,
    half,
    spread,
    folded,
    product,
    weight,
    back,
    along,
    last_rows,
    pgrad,
    land_pg,
    part,
    vec,
    land_vec,
    local_sem,
    peer_send,
    peer_recv,
    g_send,
    g_recv,
    r_send,
    r_recv,
):
    pairs = channels // 2
    me = lax.axis_index("chan")
    fr = lax.axis_index("frame")
    cx = lax.div(fr, 8)
    cy = lax.rem(lax.div(fr, 2), 4)
    cc = lax.rem(fr, 2)
    x_r, x_l = lax.rem(cx + 1, 4), lax.rem(cx + 3, 4)
    y_r, y_l = lax.rem(cy + 1, 4), lax.rem(cy + 3, 4)
    sib = 1 - cc
    dev_xr = x_r * 8 + cy * 2 + cc
    dev_xl = x_l * 8 + cy * 2 + cc
    dev_yr = cx * 8 + y_r * 2 + cc
    dev_yl = cx * 8 + y_l * 2 + cc
    dev_sib = cx * 8 + cy * 2 + sib
    core_at = cc * 16
    sib_at = sib * 16

    class Order:
        def __init__(self, major, minor, devices):
            self.col, self.col_r, self.col_l, self.col_o = [
                core_at + lax.rem(major + step, 4) * 4 for step in (0, 1, 3, 2)
            ]
            self.own, self.own_r, self.own_l, self.own_o = [
                self.col + lax.rem(minor + step, 4) for step in (0, 1, 3, 2)
            ]
            self.major_r, self.major_l, self.minor_r, self.minor_l = devices

    by_column = Order(cx, cy, (dev_xr, dev_xl, dev_yr, dev_yl))
    by_row = Order(cy, cx, (dev_yr, dev_yl, dev_xr, dev_xl))
    first_pair = channels // 2

    class Mixed:
        pass

    by_core = Mixed()
    for name, value in vars(by_column).items():
        setattr(by_core, name, cc * getattr(by_row, name) + (1 - cc) * value)

    def order(j):
        return by_column if j < first_pair else by_core

    def peer(step):
        return lax.rem(me + step, n_chan)

    def local(k, src, dst):
        copy = pltpu.make_async_copy(src, dst, local_sem.at[k])
        copy.start()
        return copy

    maps_copy = local(0, maps_hbm, maps)
    coeffs_copy = local(1, coeffs_hbm, coeffs)
    obj_copies = [
        local(2, objects_hbm.at[pl.ds(0, 2)], obj.at[pl.ds(0, 2), by_column.own]),
        local(7, objects_hbm.at[pl.ds(2, 2)], obj.at[pl.ds(2, 2), by_core.own]),
    ]
    scale_copy = local(3, scale_hbm, scale)
    amp_copy = local(4, amp_hbm, amp)
    tab_copy = local(5, table_hbm, tab)
    img_copy = local(6, images_hbm, img)
    barrier = pltpu.get_barrier_semaphore()
    for dev in (dev_yr, dev_yl, dev_xr, dev_xl, dev_sib):
        pl.semaphore_signal(barrier, inc=1, device_id={"frame": dev}, device_id_type=MESH)
    for step in range(1, n_chan):
        pl.semaphore_signal(barrier, inc=1, device_id={"chan": peer(step)}, device_id_type=MESH)

    maps_copy.wait()
    coeffs_copy.wait()
    mine = coeffs[0, 0] * maps[0]
    for m in range(1, modes):
        mine = mine + coeffs[0, m] * maps[m]
    phases[me] = mine
    for copy in obj_copies:
        copy.wait()
    pl.semaphore_wait(barrier, 5 + n_chan - 1)

    def frame_copy(src, dst, send, recv, dev):
        return pltpu.make_async_remote_copy(
            src_ref=src,
            dst_ref=dst,
            send_sem=send,
            recv_sem=recv,
            device_id={"frame": dev},
            device_id_type=MESH,
        )

    def chan_copy(src, dst, phase, dev):
        return pltpu.make_async_remote_copy(
            src_ref=src,
            dst_ref=dst,
            send_sem=peer_send.at[phase],
            recv_sem=peer_recv.at[phase],
            device_id={"chan": dev},
            device_id_type=MESH,
        )

    def gather_start(j, stage):
        o = order(j)
        across = []
        if stage == 0:
            sent = [(obj.at[j, o.own], o.minor_r), (obj.at[j, o.own], o.minor_l)]
        elif stage == 1:
            sent = [(obj.at[j, o.own_l, 0], o.minor_r), (obj.at[j, o.own_r, 1], o.minor_l)]
        elif stage == 2:
            sent = [(obj.at[j, pl.ds(o.col, 4)], o.major_r), (obj.at[j, pl.ds(o.col, 4)], o.major_l)]
            across = [o.col]
        elif stage == 3:
            sent = [
                (obj.at[j, pl.ds(o.col_l, 2)], o.major_r),
                (obj.at[j, pl.ds(o.col_r + 2, 2)], o.major_l),
            ]
            across = [o.col_r, o.col_l]
        else:
            sent = []
            across = [o.col_o]
        for src, dev in sent:
            frame_copy(src, src, g_send.at[j], g_recv.at[j, stage], dev).start()
        for col in across:
            src = obj.at[j, pl.ds(col, 4)]
            frame_copy(src, src, g_send.at[j], g_recv.at[j, 4], dev_sib).start()

    def gather_wait(j, stage):
        blocks = obj.at[j, pl.ds(0, (2, 1, 8, 4, 16)[stage])]
        frame_copy(blocks, blocks, g_send.at[j], g_recv.at[j, stage], dev_sib).wait_recv()

    def gather_next(j, stage):
        gather_wait(j, stage)
        gather_start(j, stage + 1)

    groups = ((0, 2), (2, 2))

    def reduce_start(g, stage):
        first, count = groups[g]
        o = order(first)
        here = pl.ds(first, count)
        if stage == 0:
            sent = [
                (term.at[here, pl.ds(sib_at + col, 4)], land_a.at[here, pl.ds(col, 4)], dev_sib)
                for col in [at - core_at for at in (o.col_o, o.col_r, o.col_l, o.col)]
            ]
        elif stage == 1:
            sent = [
                (term.at[here, pl.ds(o.col_o, 2)], land_b1.at[0, here], o.major_r),
                (term.at[here, pl.ds(o.col_o + 2, 2)], land_b1.at[1, here], o.major_l),
            ]
        elif stage == 2:
            sent = [
                (term.at[here, pl.ds(o.col_r, 4)], land_b2.at[0, here], o.major_r),
                (term.at[here, pl.ds(o.col_l, 4)], land_b2.at[1, here], o.major_l),
            ]
        elif stage == 3:
            sent = [
                (term.at[here, o.own_o, 0], land_c1.at[0, here], o.minor_r),
                (term.at[here, o.own_o, 1], land_c1.at[1, here], o.minor_l),
            ]
        else:
            sent = [
                (term.at[here, o.own_r], land_c2.at[0, here], o.minor_r),
                (term.at[here, o.own_l], land_c2.at[1, here], o.minor_l),
            ]
        for src, land, dev in sent:
            frame_copy(src, land, r_send.at[g], r_recv.at[g, stage], dev).start()

    def reduce_finish(g, stage):
        first, count = groups[g]
        o = order(first)
        here = pl.ds(first, count)
        blocks = term.at[here, pl.ds(0, (16, 4, 8, 1, 2)[stage])]
        frame_copy(blocks, blocks, r_send.at[g], r_recv.at[g, stage], dev_sib).wait_recv()
        for j in range(first, first + count):
            if stage == 0:
                at = pl.ds(core_at, 16)
                term[j, at] = term[j, at] + land_a[j]
            elif stage == 1:
                there, other = pl.ds(o.col_r, 2), pl.ds(o.col_l + 2, 2)
                term[j, there] = term[j, there] + land_b1[0, j]
                term[j, other] = term[j, other] + land_b1[1, j]
            elif stage == 2:
                at = pl.ds(o.col, 4)
                term[j, at] = term[j, at] + (land_b2[0, j] + land_b2[1, j])
            elif stage == 3:
                term[j, o.own_r, 0] = term[j, o.own_r, 0] + land_c1[0, j]
                term[j, o.own_l, 1] = term[j, o.own_l, 1] + land_c1[1, j]
            else:
                grad_ref[j] = term[j, o.own] + (land_c2[0, j] + land_c2[1, j])

    def reduce_next(g, stage):
        reduce_finish(g, stage)
        reduce_start(g, stage + 1)

    def each_peer(body):
        def run(step, carry):
            body(step)
            return carry

        lax.fori_loop(1, n_chan, run, 0)

    def peers_wait(phase, blocks, sent):
        copy = chan_copy(blocks, blocks, phase, peer(1))
        if sent:
            copy.wait_send()
        else:
            copy.wait_recv()

    others = pl.ds(0, n_chan - 1)
    each_peer(lambda step: chan_copy(phases.at[me], phases.at[me], 0, peer(step)).start())
    sequence = (0, 2, 1, 3)
    for j in sequence:
        gather_start(j, 0)

    amp_copy.wait()
    scale_copy.wait()
    line = lax.broadcasted_iota(jnp.int32, (PUPIL, PUPIL), 0).astype(F32) - (PUPIL - 1) / 2.0
    column = lax.broadcasted_iota(jnp.int32, (PUPIL, PUPIL), 1).astype(F32) - (PUPIL - 1) / 2.0
    inside = line * line + column * column <= (PUPIL / 2.0) ** 2
    aperture = jnp.where(inside, amp[...], 0.0)
    total = jnp.sum(aperture * aperture, axis=(0, 1), keepdims=True)
    inverse = 1.0 / (total * float(GRID * GRID))

    for stage in (0, 1):
        for j in sequence:
            gather_next(j, stage)
    peers_wait(0, phases.at[others], False)
    tab_copy.wait()

    def table(k):
        return tab[0, k].astype(BF16), tab[1, k].astype(BF16)

    def each_channel(body):
        def run(j, carry):
            body(j)
            return carry

        lax.fori_loop(0, channels, run, 0)

    def each_half(body):
        def run(i, carry):
            body(lax.div(i, 2), lax.rem(i, 2))
            return carry

        lax.fori_loop(0, 2 * channels, run, 0)

    wave = phases[...].reshape(PUPIL, PUPIL)

    def fields(j):
        sin_v, cos_v = sincos(scale[j] * wave)
        real, imag = aperture * cos_v, aperture * sin_v
        pupil[j, :, 0:PUPIL] = real
        pupil[j, :, PUPIL:GRID] = imag

    each_channel(fields)

    def pupil_rows(j):
        x_hi, x_lo = split(pupil[j])
        real = dot3(x_hi, x_lo, *table(T_A))
        imag = dot3(x_hi, x_lo, *table(T_B))
        half[j, 0, 0:PUPIL, :] = real
        half[j, 0, PUPIL:GRID, :] = imag
        half[j, 1, 0:PUPIL, :] = imag
        half[j, 1, PUPIL:GRID, :] = -real

    each_channel(pupil_rows)
    gather_next(0, 2)
    gather_next(2, 2)

    def to_spread(j, n):
        spread[j, n] = dot3(*table(T_L2), *split(half[j, n]))

    each_half(to_spread)
    gather_next(1, 2)
    gather_next(3, 2)
    gather_next(0, 3)

    def fold(j):
        real, imag = spread[j, 0], spread[j, 1]
        folded[j] = dot3(*split((real * real + imag * imag) * inverse), *table(T_H))

    each_channel(fold)
    gather_next(2, 3)
    gather_next(1, 3)

    def products(j, t):
        product[j, t] = dot3(*table(T_C + t), *split(folded[j]))

    each_half(products)
    gather_next(3, 3)
    img_copy.wait()

    lane0 = lax.broadcasted_iota(jnp.int32, (16, PUPIL), 1) == 0

    def residual_block(p, s, b):
        j = 2 * p + s
        at = pl.ds(pl.multiple_of(b * 16, 16), 16)
        crossed = lax.rem(b, 4) * 4 + lax.div(b, 4)
        k = 16 + p * crossed + (1 - p) * b
        o_r = jnp.concatenate([obj[j, b, 0], obj[j, k, 0]], 0)
        o_i = jnp.concatenate([obj[j, b, 1], obj[j, k, 1]], 0)
        p1, p3 = product[j, 0, at, 0:PUPIL], product[j, 0, at, PUPIL:GRID]
        p4, p2 = product[j, 1, at, 0:PUPIL], product[j, 1, at, PUPIL:GRID]
        t_r = jnp.concatenate(
            [p1 + jnp.where(lane0, 0.0, p2), mirror(jnp.where(lane0, p3, p1 - p2))], 1
        )
        t_i = jnp.concatenate(
            [jnp.where(lane0, 0.0, p3) - p4, mirror(jnp.where(lane0, -p2, -p3 - p4))], 1
        )
        r_r = o_r * t_r - o_i * t_i - img[j, 0, 0, at, :]
        r_i = o_r * t_i + o_i * t_r - img[j, 0, 1, at, :]
        g_r = t_r * r_r + t_i * r_i
        g_i = t_r * r_i - t_i * r_r
        term[j, b, 0] = g_r[0:8]
        term[j, k, 0] = g_r[8:16]
        term[j, b, 1] = g_i[0:8]
        term[j, k, 1] = g_i[8:16]
        w_r = o_r * r_r + o_i * r_i
        w_i = o_r * r_i - o_i * r_r
        wr_p, wi_p = w_r[:, 0:PUPIL], w_i[:, 0:PUPIL]
        wr_m, wi_m = mirror(w_r[:, PUPIL:GRID]), mirror(w_i[:, PUPIL:GRID])
        top = jnp.concatenate(
            [wr_p + jnp.where(lane0, 0.0, wr_m), jnp.where(lane0, wr_m, wi_p - wi_m)], 1
        )
        low = jnp.concatenate(
            [-(wi_p + jnp.where(lane0, 0.0, wi_m)), jnp.where(lane0, -wi_m, wr_p - wr_m)], 1
        )
        weight[j, 0, at, :] = top
        weight[j, 1, at, :] = low

    def residual(p):
        def run(b, carry):
            for s in range(2):
                residual_block(p, s, b)
            return carry

        lax.fori_loop(0, GRID // 16, run, 0, unroll=2)

    def pair_residual(p, carry):
        gather_wait(2 * p, 4)
        gather_wait(2 * p + 1, 4)
        residual(p)

        @pl.when(p == 0)
        def _():
            reduce_start(0, 0)

        @pl.when(p == 1)
        def _():
            reduce_start(1, 0)

        return carry

    lax.fori_loop(0, pairs, pair_residual, 0)

    def unproducts(j, t):
        back[j, t] = dot3(*table(T_C + t), *split(weight[j, t]))

    each_half(unproducts)
    reduce_next(0, 0)

    def unfold(j):
        change = dot3(*split(back[j, 0] + back[j, 1]), *table(T_HT)) * (2.0 * inverse)
        along[j, 0] = change * spread[j, 0]
        along[j, 1] = change * spread[j, 1]

    each_channel(unfold)
    reduce_next(1, 0)
    reduce_next(0, 1)

    def from_spread(j, n):
        last_rows[j, n] = dot3(*split(along[j, n]), *table(T_BACK + n))

    each_half(from_spread)
    reduce_next(1, 1)
    reduce_next(0, 2)
    pgrad[...] = jnp.zeros_like(pgrad)

    def to_pupil(j):
        g = dot3(*table(T_A), *split(last_rows[j, 0] + last_rows[j, 1]))
        g_r = g[0:PUPIL, 0:PUPIL] - g[PUPIL:GRID, PUPIL:GRID]
        g_i = g[PUPIL:GRID, 0:PUPIL] + g[0:PUPIL, PUPIL:GRID]
        change = scale[j] * (pupil[j, :, 0:PUPIL] * g_i - pupil[j, :, PUPIL:GRID] * g_r)
        pgrad[...] = pgrad[...] + change.reshape(pgrad.shape)

    each_channel(to_pupil)
    each_peer(lambda step: chan_copy(pgrad.at[peer(step)], land_pg.at[step], 1, peer(step)).start())
    reduce_next(0, 3)
    reduce_next(1, 2)

    part[...] = jnp.zeros_like(part)
    peers_wait(1, land_pg.at[others], False)
    summed = pgrad[me]
    for step in range(1, n_chan):
        summed = summed + land_pg[step]
    for m in range(modes):
        part[m : m + 1, :] = jnp.sum(maps[m] * summed, axis=0, keepdims=True)
    vec[...] = lax.dot_general(
        jnp.ones((8, PUPIL), F32),
        part[...],
        (((1,), (1,)), ((), ())),
        precision=lax.Precision.HIGHEST,
        preferred_element_type=F32,
    )
    each_peer(lambda step: chan_copy(vec, land_vec.at[step], 2, peer(step)).start())
    reduce_next(1, 3)
    reduce_finish(0, 4)
    peers_wait(2, land_vec.at[others], False)
    answer = vec[...]
    for step in range(1, n_chan):
        answer = answer + land_vec[step]
    mode_ref[...] = answer[0:1, 0:modes]
    reduce_finish(1, 4)

    for j in range(channels):
        blocks = obj.at[j, pl.ds(0, 31)]
        frame_copy(blocks, blocks, g_send.at[j], g_recv.at[j, 0], dev_sib).wait_send()
    for g, (first, count) in enumerate(groups):
        blocks = term.at[pl.ds(first, count), pl.ds(0, 31)]
        frame_copy(blocks, blocks, r_send.at[g], r_recv.at[g, 0], dev_sib).wait_send()
    peers_wait(0, phases.at[others], True)
    peers_wait(1, land_pg.at[others], True)
    peers_wait(2, land_vec.at[others], True)


def on_device(n_chan, images, objects, coeffs, mode_maps, amplitude, phase_scale):
    channels = images.shape[0]
    modes = coeffs.shape[1]
    rows = mode_maps.shape[1]
    vmem = pl.BlockSpec(memory_space=pltpu.VMEM)
    hbm = pl.BlockSpec(memory_space=pltpu.HBM)
    dma = pltpu.SemaphoreType.DMA
    block = (2, 8, GRID)
    outs = (
        jax.ShapeDtypeStruct(objects.shape, F32),
        jax.ShapeDtypeStruct(coeffs.shape, F32),
    )
    inputs = (images, objects, coeffs, mode_maps, amplitude, phase_scale, jnp.asarray(build_tables()))
    return pl.pallas_call(
        functools.partial(kernel, n_chan, channels, modes),
        out_shape=outs,
        in_specs=[hbm] * 7,
        out_specs=(vmem, vmem),
        scratch_shapes=[
            pltpu.SMEM(coeffs.shape, F32),
            pltpu.SMEM(phase_scale.shape, F32),
            pltpu.VMEM(mode_maps.shape, F32),
            pltpu.VMEM(amplitude.shape, F32),
            pltpu.VMEM(images.shape, F32),
            pltpu.VMEM((2, 9, GRID, GRID), F32),
            pltpu.VMEM((channels, 32) + block, F32),
            pltpu.VMEM((channels, 32) + block, F32),
            pltpu.VMEM((channels, 16) + block, F32),
            pltpu.VMEM((2, channels, 2) + block, F32),
            pltpu.VMEM((2, channels, 4) + block, F32),
            pltpu.VMEM((2, channels, 8, GRID), F32),
            pltpu.VMEM((2, channels) + block, F32),
            pltpu.VMEM((n_chan, rows, PUPIL), F32),
            pltpu.VMEM((channels, PUPIL, GRID), F32),
            pltpu.VMEM((channels, 2, GRID, GRID), F32),
            pltpu.VMEM((channels, 2, GRID, GRID), F32),
            pltpu.VMEM((channels, GRID, GRID), F32),
            pltpu.VMEM((channels, 2, GRID, GRID), F32),
            pltpu.VMEM((channels, 2, GRID, GRID), F32),
            pltpu.VMEM((channels, 2, GRID, GRID), F32),
            pltpu.VMEM((channels, 2, GRID, GRID), F32),
            pltpu.VMEM((channels, 2, GRID, GRID), F32),
            pltpu.VMEM((n_chan, rows, PUPIL), F32),
            pltpu.VMEM((n_chan, rows, PUPIL), F32),
            pltpu.VMEM((PUPIL, PUPIL), F32),
            pltpu.VMEM((8, PUPIL), F32),
            pltpu.VMEM((n_chan, 8, PUPIL), F32),
            dma((8,)),
            dma((3,)),
            dma((3,)),
            dma((channels,)),
            dma((channels, 5)),
            dma((3,)),
            dma((3, 5)),
        ],
        compiler_params=pltpu.CompilerParams(
            collective_id=0, has_side_effects=True, vmem_limit_bytes=48 * 1024 * 1024
        ),
        name="deconvolve",
    )(*[pltpu.with_memory_space_constraint(value, pltpu.HBM) for value in inputs])


def solution(mesh):
    return jax.shard_map(
        functools.partial(on_device, mesh.shape["chan"]),
        mesh=mesh,
        in_specs=(
            P("chan", "frame", None, None, None),
            P("chan", None, "frame", None),
            P("frame", None),
            P(None, "chan", None),
            P(),
            P("chan"),
        ),
        out_specs=(P("chan", None, "frame", None), P("frame", None)),
        check_vma=False,
    )
```

```python
import functools
import math

import jax
import jax.numpy as jnp
import ml_dtypes
import numpy as np
from jax import lax
from jax.experimental import pallas as pl
from jax.experimental.pallas import tpu as pltpu
from jax.sharding import PartitionSpec as P

F32 = jnp.float32
BF16 = jnp.bfloat16
MESH = pl.DeviceIdType.MESH
GRID = 256
PUPIL = 128

T_A, T_B, T_L2, T_H, T_C, T_S, T_HT, T_BACK = 0, 1, 2, 3, 4, 5, 6, 7


def build_tables():
    index = np.arange(GRID)
    turn = (np.outer(index, index) % GRID) * (2.0 * math.pi / GRID)
    cos, sin = np.cos(turn), np.sin(turn)
    half = PUPIL
    first = np.concatenate([cos[:half], sin[:half]], 0)
    second = np.concatenate([-sin[:half], cos[:half]], 0)
    left = np.concatenate([cos[:, :half], sin[:, :half]], 1)
    minus = -sin[:, :half]
    minus[:, 0] = cos[:, half]
    herm = np.concatenate([cos[:, :half], minus], 1)
    back = np.concatenate(
        [
            np.concatenate([cos[:, :half], sin[:, :half]], 1),
            np.concatenate([-sin[:, :half], cos[:, :half]], 1),
        ],
        0,
    )
    table = np.concatenate([first, second, left, herm, cos, sin, herm.T, back], 0).astype(np.float32)
    high = table.astype(ml_dtypes.bfloat16)
    high = high.astype(np.float32)
    low = (table - high).astype(ml_dtypes.bfloat16).astype(np.float32)
    return np.stack([high, low]).reshape(2, -1, GRID, GRID)


def split(value):
    high = value.astype(BF16)
    low = (value - high.astype(F32)).astype(BF16)
    return high, low


def dot(a, b):
    return jnp.dot(a, b, preferred_element_type=F32)


def dot3(a_high, a_low, b_high, b_low):
    left = jnp.concatenate([a_high, a_low, a_high], 1)
    right = jnp.concatenate([b_high, b_high, b_low], 0)
    return dot(left, right)


def sincos(angle):
    k = jnp.floor(angle * (2.0 / math.pi) + 0.5)
    r = ((angle - k * 1.5703125) - k * 4.837512969970703125e-4) - k * 7.54978995489188216e-8
    z = r * r
    sin_r = ((-1.9515295891e-4 * z + 8.3321608736e-3) * z - 1.6666654611e-1) * z * r + r
    cos_r = ((2.443315711809948e-5 * z - 1.388731625493765e-3) * z + 4.166664568298827e-2) * z * z - 0.5 * z + 1.0
    quad = k - 4.0 * jnp.floor(k * 0.25)
    odd = (quad == 1.0) | (quad == 3.0)
    sin_v = jnp.where(odd, cos_r, sin_r)
    cos_v = jnp.where(odd, sin_r, cos_r)
    sin_v = jnp.where(quad >= 2.0, -sin_v, sin_v)
    cos_v = jnp.where((quad == 1.0) | (quad == 2.0), -cos_v, cos_v)
    return sin_v, cos_v


def mirror(value):
    lane = lax.broadcasted_iota(jnp.int32, value.shape, 1)
    index = (PUPIL - lane) & (PUPIL - 1)
    return jnp.take_along_axis(value, index, axis=1, mode="promise_in_bounds")


def kernel(
    n_chan,
    channels,
    modes,
    images_hbm,
    objects_hbm,
    coeffs_hbm,
    maps_hbm,
    amp_hbm,
    scale_hbm,
    table_hbm,
    grad_ref,
    mode_ref,
    coeffs,
    scale,
    maps,
    amp,
    img,
    tab,
    obj,
    term,
    land_a,
    land_b1,
    land_b2,
    land_c1,
    land_c2,
    phases,
    pupil,
    half,
    spread,
    folded,
    product,
    weight,
    back,
    along,
    last_rows,
    pgrad,
    land_pg,
    part,
    vec,
    land_vec,
    local_sem,
    peer_send,
    peer_recv,
    g_send,
    g_recv,
    r_send,
    r_recv,
):
    pairs = channels // 2
    me = lax.axis_index("chan")
    fr = lax.axis_index("frame")
    cx = lax.div(fr, 8)
    cy = lax.rem(lax.div(fr, 2), 4)
    cc = lax.rem(fr, 2)
    x_r, x_l = lax.rem(cx + 1, 4), lax.rem(cx + 3, 4)
    y_r, y_l = lax.rem(cy + 1, 4), lax.rem(cy + 3, 4)
    sib = 1 - cc
    dev_xr = x_r * 8 + cy * 2 + cc
    dev_xl = x_l * 8 + cy * 2 + cc
    dev_yr = cx * 8 + y_r * 2 + cc
    dev_yl = cx * 8 + y_l * 2 + cc
    dev_sib = cx * 8 + cy * 2 + sib
    core_at = cc * 16
    sib_at = sib * 16

    class Order:
        def __init__(self, major, minor, devices):
            self.col, self.col_r, self.col_l, self.col_o = [
                core_at + lax.rem(major + step, 4) * 4 for step in (0, 1, 3, 2)
            ]
            self.own, self.own_r, self.own_l, self.own_o = [
                self.col + lax.rem(minor + step, 4) for step in (0, 1, 3, 2)
            ]
            self.major_r, self.major_l, self.minor_r, self.minor_l = devices

    by_column = Order(cx, cy, (dev_xr, dev_xl, dev_yr, dev_yl))
    by_row = Order(cy, cx, (dev_yr, dev_yl, dev_xr, dev_xl))
    class Mixed:
        pass

    by_core = Mixed()
    for name, value in vars(by_column).items():
        setattr(by_core, name, cc * getattr(by_row, name) + (1 - cc) * value)

    def order(j):
        return by_column if j == 0 else by_core

    def peer(step):
        return lax.rem(me + step, n_chan)

    def local(k, src, dst):
        copy = pltpu.make_async_copy(src, dst, local_sem.at[k])
        copy.start()
        return copy

    maps_copy = local(0, maps_hbm, maps)
    coeffs_copy = local(1, coeffs_hbm, coeffs)
    obj_copies = [
        local(2, objects_hbm.at[pl.ds(0, 1)], obj.at[pl.ds(0, 1), by_column.own]),
        local(7, objects_hbm.at[pl.ds(1, 3)], obj.at[pl.ds(1, 3), by_core.own]),
    ]
    scale_copy = local(3, scale_hbm, scale)
    amp_copy = local(4, amp_hbm, amp)
    tab_copy = local(5, table_hbm, tab)
    img_copy = local(6, images_hbm, img)
    barrier = pltpu.get_barrier_semaphore()
    for dev in (dev_yr, dev_yl, dev_xr, dev_xl, dev_sib):
        pl.semaphore_signal(barrier, inc=1, device_id={"frame": dev}, device_id_type=MESH)
    for step in range(1, n_chan):
        pl.semaphore_signal(barrier, inc=1, device_id={"chan": peer(step)}, device_id_type=MESH)

    maps_copy.wait()
    coeffs_copy.wait()
    mine = coeffs[0, 0] * maps[0]
    for m in range(1, modes):
        mine = mine + coeffs[0, m] * maps[m]
    phases[me] = mine
    for copy in obj_copies:
        copy.wait()
    pl.semaphore_wait(barrier, 5 + n_chan - 1)

    def frame_copy(src, dst, send, recv, dev):
        return pltpu.make_async_remote_copy(
            src_ref=src,
            dst_ref=dst,
            send_sem=send,
            recv_sem=recv,
            device_id={"frame": dev},
            device_id_type=MESH,
        )

    def chan_copy(src, dst, phase, dev):
        return pltpu.make_async_remote_copy(
            src_ref=src,
            dst_ref=dst,
            send_sem=peer_send.at[phase],
            recv_sem=peer_recv.at[phase],
            device_id={"chan": dev},
            device_id_type=MESH,
        )

    def gather_start(j, stage):
        o = order(j)
        across = []
        if stage == 0:
            sent = [(obj.at[j, o.own], o.minor_r), (obj.at[j, o.own], o.minor_l)]
        elif stage == 1:
            sent = [(obj.at[j, o.own_l, 0], o.minor_r), (obj.at[j, o.own_r, 1], o.minor_l)]
        elif stage == 2:
            sent = [(obj.at[j, pl.ds(o.col, 4)], o.major_r), (obj.at[j, pl.ds(o.col, 4)], o.major_l)]
            across = [o.col]
        elif stage == 3:
            sent = [
                (obj.at[j, pl.ds(o.col_l, 2)], o.major_r),
                (obj.at[j, pl.ds(o.col_r + 2, 2)], o.major_l),
            ]
            across = [o.col_r, o.col_l]
        else:
            sent = []
            across = [o.col_o]
        for src, dev in sent:
            frame_copy(src, src, g_send.at[j], g_recv.at[j, stage], dev).start()
        for col in across:
            src = obj.at[j, pl.ds(col, 4)]
            frame_copy(src, src, g_send.at[j], g_recv.at[j, 4], dev_sib).start()

    def gather_wait(j, stage):
        blocks = obj.at[j, pl.ds(0, (2, 1, 8, 4, 16)[stage])]
        frame_copy(blocks, blocks, g_send.at[j], g_recv.at[j, stage], dev_sib).wait_recv()

    def gather_next(j, stage):
        gather_wait(j, stage)
        gather_start(j, stage + 1)

    groups = ((0, 1), (1, 1), (2, 2))

    def reduce_start(g, stage):
        first, count = groups[g]
        o = order(first)
        here = pl.ds(first, count)
        if stage == 0:
            sent = [
                (term.at[here, pl.ds(sib_at + col, 4)], land_a.at[here, pl.ds(col, 4)], dev_sib)
                for col in [at - core_at for at in (o.col_o, o.col_r, o.col_l, o.col)]
            ]
        elif stage == 1:
            sent = [
                (term.at[here, pl.ds(o.col_o, 2)], land_b1.at[0, here], o.major_r),
                (term.at[here, pl.ds(o.col_o + 2, 2)], land_b1.at[1, here], o.major_l),
            ]
        elif stage == 2:
            sent = [
                (term.at[here, pl.ds(o.col_r, 4)], land_b2.at[0, here], o.major_r),
                (term.at[here, pl.ds(o.col_l, 4)], land_b2.at[1, here], o.major_l),
            ]
        elif stage == 3:
            sent = [
                (term.at[here, o.own_o, 0], land_c1.at[0, here], o.minor_r),
                (term.at[here, o.own_o, 1], land_c1.at[1, here], o.minor_l),
            ]
        else:
            sent = [
                (term.at[here, o.own_r], land_c2.at[0, here], o.minor_r),
                (term.at[here, o.own_l], land_c2.at[1, here], o.minor_l),
            ]
        for src, land, dev in sent:
            frame_copy(src, land, r_send.at[g], r_recv.at[g, stage], dev).start()

    def reduce_finish(g, stage):
        first, count = groups[g]
        o = order(first)
        here = pl.ds(first, count)
        blocks = term.at[here, pl.ds(0, (16, 4, 8, 1, 2)[stage])]
        frame_copy(blocks, blocks, r_send.at[g], r_recv.at[g, stage], dev_sib).wait_recv()
        for j in range(first, first + count):
            if stage == 0:
                at = pl.ds(core_at, 16)
                term[j, at] = term[j, at] + land_a[j]
            elif stage == 1:
                there, other = pl.ds(o.col_r, 2), pl.ds(o.col_l + 2, 2)
                term[j, there] = term[j, there] + land_b1[0, j]
                term[j, other] = term[j, other] + land_b1[1, j]
            elif stage == 2:
                at = pl.ds(o.col, 4)
                term[j, at] = term[j, at] + (land_b2[0, j] + land_b2[1, j])
            elif stage == 3:
                term[j, o.own_r, 0] = term[j, o.own_r, 0] + land_c1[0, j]
                term[j, o.own_l, 1] = term[j, o.own_l, 1] + land_c1[1, j]
            else:
                grad_ref[j] = term[j, o.own] + (land_c2[0, j] + land_c2[1, j])

    def reduce_next(g, stage):
        reduce_finish(g, stage)
        reduce_start(g, stage + 1)

    def each_peer(body):
        def run(step, carry):
            body(step)
            return carry

        lax.fori_loop(1, n_chan, run, 0)

    def peers_wait(phase, blocks, sent):
        copy = chan_copy(blocks, blocks, phase, peer(1))
        if sent:
            copy.wait_send()
        else:
            copy.wait_recv()

    others = pl.ds(0, n_chan - 1)
    each_peer(lambda step: chan_copy(phases.at[me], phases.at[me], 0, peer(step)).start())
    sequence = (0, 2, 1, 3)
    for j in sequence:
        gather_start(j, 0)

    amp_copy.wait()
    scale_copy.wait()
    line = lax.broadcasted_iota(jnp.int32, (PUPIL, PUPIL), 0).astype(F32) - (PUPIL - 1) / 2.0
    column = lax.broadcasted_iota(jnp.int32, (PUPIL, PUPIL), 1).astype(F32) - (PUPIL - 1) / 2.0
    inside = line * line + column * column <= (PUPIL / 2.0) ** 2
    aperture = jnp.where(inside, amp[...], 0.0)
    total = jnp.sum(aperture * aperture, axis=(0, 1), keepdims=True)
    inverse = 1.0 / (total * float(GRID * GRID))

    for stage in (0, 1):
        for j in sequence:
            gather_next(j, stage)
    peers_wait(0, phases.at[others], False)
    tab_copy.wait()

    def table(k):
        return tab[0, k].astype(BF16), tab[1, k].astype(BF16)

    def each_channel(body):
        def run(j, carry):
            body(j)
            return carry

        lax.fori_loop(0, channels, run, 0)

    def each_half(body):
        def run(i, carry):
            body(lax.div(i, 2), lax.rem(i, 2))
            return carry

        lax.fori_loop(0, 2 * channels, run, 0)

    wave = phases[...].reshape(PUPIL, PUPIL)

    def fields(j):
        sin_v, cos_v = sincos(scale[j] * wave)
        real, imag = aperture * cos_v, aperture * sin_v
        pupil[j, :, 0:PUPIL] = real
        pupil[j, :, PUPIL:GRID] = imag

    each_channel(fields)

    def pupil_rows(j):
        x_hi, x_lo = split(pupil[j])
        real = dot3(x_hi, x_lo, *table(T_A))
        imag = dot3(x_hi, x_lo, *table(T_B))
        half[j, 0, 0:PUPIL, :] = real
        half[j, 0, PUPIL:GRID, :] = imag
        half[j, 1, 0:PUPIL, :] = imag
        half[j, 1, PUPIL:GRID, :] = -real

    each_channel(pupil_rows)
    gather_next(0, 2)
    gather_next(2, 2)

    def to_spread(j, n):
        spread[j, n] = dot3(*table(T_L2), *split(half[j, n]))

    each_half(to_spread)
    gather_next(1, 2)
    gather_next(3, 2)
    gather_next(0, 3)

    def fold(j):
        real, imag = spread[j, 0], spread[j, 1]
        folded[j] = dot3(*split((real * real + imag * imag) * inverse), *table(T_H))

    each_channel(fold)
    gather_next(2, 3)
    gather_next(1, 3)

    def products(j, t):
        product[j, t] = dot3(*table(T_C + t), *split(folded[j]))

    each_half(products)
    gather_next(3, 3)
    img_copy.wait()

    lane0 = lax.broadcasted_iota(jnp.int32, (16, PUPIL), 1) == 0

    def residual_block(p, s, b):
        j = 2 * p + s
        at = pl.ds(pl.multiple_of(b * 16, 16), 16)
        crossed = lax.rem(b, 4) * 4 + lax.div(b, 4)
        k = 16 + (crossed if s == 1 else p * crossed + (1 - p) * b)
        o_r = jnp.concatenate([obj[j, b, 0], obj[j, k, 0]], 0)
        o_i = jnp.concatenate([obj[j, b, 1], obj[j, k, 1]], 0)
        p1, p3 = product[j, 0, at, 0:PUPIL], product[j, 0, at, PUPIL:GRID]
        p4, p2 = product[j, 1, at, 0:PUPIL], product[j, 1, at, PUPIL:GRID]
        t_r = jnp.concatenate(
            [p1 + jnp.where(lane0, 0.0, p2), mirror(jnp.where(lane0, p3, p1 - p2))], 1
        )
        t_i = jnp.concatenate(
            [jnp.where(lane0, 0.0, p3) - p4, mirror(jnp.where(lane0, -p2, -p3 - p4))], 1
        )
        r_r = o_r * t_r - o_i * t_i - img[j, 0, 0, at, :]
        r_i = o_r * t_i + o_i * t_r - img[j, 0, 1, at, :]
        g_r = t_r * r_r + t_i * r_i
        g_i = t_r * r_i - t_i * r_r
        term[j, b, 0] = g_r[0:8]
        term[j, k, 0] = g_r[8:16]
        term[j, b, 1] = g_i[0:8]
        term[j, k, 1] = g_i[8:16]
        w_r = o_r * r_r + o_i * r_i
        w_i = o_r * r_i - o_i * r_r
        wr_p, wi_p = w_r[:, 0:PUPIL], w_i[:, 0:PUPIL]
        wr_m, wi_m = mirror(w_r[:, PUPIL:GRID]), mirror(w_i[:, PUPIL:GRID])
        top = jnp.concatenate(
            [wr_p + jnp.where(lane0, 0.0, wr_m), jnp.where(lane0, wr_m, wi_p - wi_m)], 1
        )
        low = jnp.concatenate(
            [-(wi_p + jnp.where(lane0, 0.0, wi_m)), jnp.where(lane0, -wi_m, wr_p - wr_m)], 1
        )
        weight[j, 0, at, :] = top
        weight[j, 1, at, :] = low

    def residual(p):
        def run(b, carry):
            for s in range(2):
                residual_block(p, s, b)
            return carry

        lax.fori_loop(0, GRID // 16, run, 0, unroll=2)

    def pair_residual(p, carry):
        gather_wait(2 * p, 4)
        gather_wait(2 * p + 1, 4)
        residual(p)

        @pl.when(p == 0)
        def _():
            reduce_start(0, 0)
            reduce_start(1, 0)

        @pl.when(p == 1)
        def _():
            reduce_start(2, 0)

        return carry

    lax.fori_loop(0, pairs, pair_residual, 0)

    def unproducts(j, t):
        back[j, t] = dot3(*table(T_C + t), *split(weight[j, t]))

    each_half(unproducts)
    reduce_next(0, 0)
    reduce_next(1, 0)

    def unfold(j):
        change = dot3(*split(back[j, 0] + back[j, 1]), *table(T_HT)) * (2.0 * inverse)
        along[j, 0] = change * spread[j, 0]
        along[j, 1] = change * spread[j, 1]

    each_channel(unfold)
    reduce_next(2, 0)
    reduce_next(0, 1)
    reduce_next(1, 1)

    def from_spread(j, n):
        last_rows[j, n] = dot3(*split(along[j, n]), *table(T_BACK + n))

    each_half(from_spread)
    reduce_next(2, 1)
    reduce_next(0, 2)
    reduce_next(1, 2)
    pgrad[...] = jnp.zeros_like(pgrad)

    def to_pupil(j):
        g = dot3(*table(T_A), *split(last_rows[j, 0] + last_rows[j, 1]))
        g_r = g[0:PUPIL, 0:PUPIL] - g[PUPIL:GRID, PUPIL:GRID]
        g_i = g[PUPIL:GRID, 0:PUPIL] + g[0:PUPIL, PUPIL:GRID]
        change = scale[j] * (pupil[j, :, 0:PUPIL] * g_i - pupil[j, :, PUPIL:GRID] * g_r)
        pgrad[...] = pgrad[...] + change.reshape(pgrad.shape)

    each_channel(to_pupil)
    each_peer(lambda step: chan_copy(pgrad.at[peer(step)], land_pg.at[step], 1, peer(step)).start())
    reduce_next(0, 3)
    reduce_next(1, 3)
    reduce_next(2, 2)

    part[...] = jnp.zeros_like(part)
    peers_wait(1, land_pg.at[others], False)
    summed = pgrad[me]
    for step in range(1, n_chan):
        summed = summed + land_pg[step]
    for m in range(modes):
        part[m : m + 1, :] = jnp.sum(maps[m] * summed, axis=0, keepdims=True)
    vec[...] = lax.dot_general(
        jnp.ones((8, PUPIL), F32),
        part[...],
        (((1,), (1,)), ((), ())),
        precision=lax.Precision.HIGHEST,
        preferred_element_type=F32,
    )
    each_peer(lambda step: chan_copy(vec, land_vec.at[step], 2, peer(step)).start())
    reduce_next(2, 3)
    reduce_finish(0, 4)
    reduce_finish(1, 4)
    peers_wait(2, land_vec.at[others], False)
    answer = vec[...]
    for step in range(1, n_chan):
        answer = answer + land_vec[step]
    mode_ref[...] = answer[0:1, 0:modes]
    reduce_finish(2, 4)

    for j in range(channels):
        blocks = obj.at[j, pl.ds(0, 31)]
        frame_copy(blocks, blocks, g_send.at[j], g_recv.at[j, 0], dev_sib).wait_send()
    for g, (first, count) in enumerate(groups):
        blocks = term.at[pl.ds(first, count), pl.ds(0, 31)]
        frame_copy(blocks, blocks, r_send.at[g], r_recv.at[g, 0], dev_sib).wait_send()
    peers_wait(0, phases.at[others], True)
    peers_wait(1, land_pg.at[others], True)
    peers_wait(2, land_vec.at[others], True)


def on_device(n_chan, images, objects, coeffs, mode_maps, amplitude, phase_scale):
    channels = images.shape[0]
    modes = coeffs.shape[1]
    rows = mode_maps.shape[1]
    vmem = pl.BlockSpec(memory_space=pltpu.VMEM)
    hbm = pl.BlockSpec(memory_space=pltpu.HBM)
    dma = pltpu.SemaphoreType.DMA
    block = (2, 8, GRID)
    outs = (
        jax.ShapeDtypeStruct(objects.shape, F32),
        jax.ShapeDtypeStruct(coeffs.shape, F32),
    )
    inputs = (images, objects, coeffs, mode_maps, amplitude, phase_scale, jnp.asarray(build_tables()))
    return pl.pallas_call(
        functools.partial(kernel, n_chan, channels, modes),
        out_shape=outs,
        in_specs=[hbm] * 7,
        out_specs=(vmem, vmem),
        scratch_shapes=[
            pltpu.SMEM(coeffs.shape, F32),
            pltpu.SMEM(phase_scale.shape, F32),
            pltpu.VMEM(mode_maps.shape, F32),
            pltpu.VMEM(amplitude.shape, F32),
            pltpu.VMEM(images.shape, F32),
            pltpu.VMEM((2, 9, GRID, GRID), F32),
            pltpu.VMEM((channels, 32) + block, F32),
            pltpu.VMEM((channels, 32) + block, F32),
            pltpu.VMEM((channels, 16) + block, F32),
            pltpu.VMEM((2, channels, 2) + block, F32),
            pltpu.VMEM((2, channels, 4) + block, F32),
            pltpu.VMEM((2, channels, 8, GRID), F32),
            pltpu.VMEM((2, channels) + block, F32),
            pltpu.VMEM((n_chan, rows, PUPIL), F32),
            pltpu.VMEM((channels, PUPIL, GRID), F32),
            pltpu.VMEM((channels, 2, GRID, GRID), F32),
            pltpu.VMEM((channels, 2, GRID, GRID), F32),
            pltpu.VMEM((channels, GRID, GRID), F32),
            pltpu.VMEM((channels, 2, GRID, GRID), F32),
            pltpu.VMEM((channels, 2, GRID, GRID), F32),
            pltpu.VMEM((channels, 2, GRID, GRID), F32),
            pltpu.VMEM((channels, 2, GRID, GRID), F32),
            pltpu.VMEM((channels, 2, GRID, GRID), F32),
            pltpu.VMEM((n_chan, rows, PUPIL), F32),
            pltpu.VMEM((n_chan, rows, PUPIL), F32),
            pltpu.VMEM((PUPIL, PUPIL), F32),
            pltpu.VMEM((8, PUPIL), F32),
            pltpu.VMEM((n_chan, 8, PUPIL), F32),
            dma((8,)),
            dma((3,)),
            dma((3,)),
            dma((channels,)),
            dma((channels, 5)),
            dma((3,)),
            dma((3, 5)),
        ],
        compiler_params=pltpu.CompilerParams(
            collective_id=0, has_side_effects=True, vmem_limit_bytes=48 * 1024 * 1024
        ),
        name="deconvolve",
    )(*[pltpu.with_memory_space_constraint(value, pltpu.HBM) for value in inputs])


def solution(mesh):
    return jax.shard_map(
        functools.partial(on_device, mesh.shape["chan"]),
        mesh=mesh,
        in_specs=(
            P("chan", "frame", None, None, None),
            P("chan", None, "frame", None),
            P("frame", None),
            P(None, "chan", None),
            P(),
            P("chan"),
        ),
        out_specs=(P("chan", None, "frame", None), P("frame", None)),
        check_vma=False,
    )
```
